512 devices in a mesh: item: 8 (over y, x_lo), fsdp: 64 (over z, x_hi, core).
Axes of the slice: x: 4 (x_hi: 2, x_lo: 2; x = x_hi * 2 + x_lo), y: 4, z: 16, core: 2. Of those that a mesh axis runs over, the one named last changes fastest.
Arguments:
- history: bfloat16 [512, 512, 512], P(('item', 'fsdp')), may hold values from -6 to 6
- actions: int32 [512, 512], P(('item', 'fsdp')), may hold values from 0 to 15
- action_table: bfloat16 [16, 512], replicated, may hold values from -3 to 3
- w_in: bfloat16 [2, 512, 2048], P(None, 'fsdp'), may hold values from -0.25 to 0.25
- w_out: bfloat16 [2, 512, 512], P(None, 'fsdp'), may hold values from -0.25 to 0.25
- w_int: bfloat16 [512, 512], P('fsdp'), may hold values from -0.25 to 0.25
- codebook: bfloat16 [32, 256, 16], replicated, may hold values from -0.25 to 0.25
- codes: int32 [128, 128, 32], P('item'), may hold values from 0 to 255
- cand: int32 [512, 4, 8, 4], P(('item', 'fsdp')), may hold values from 0 to 15
- counts: int32 [512, 32], P(('item', 'fsdp')), may hold values from 1 to 4, 80 in all within a row
Outputs:
- scores: float32 [512, 4, 8, 4, 128], P(('item', 'fsdp'))
The draws below stay inside these ranges and needn't reach their ends.
Inputs may be any that keep to these rules, and one draw needn't show every extreme that they name: `cand`: block numbers within a group; slots at or beyond the count hold ids that are not read. For each user the counts over all 32 columns sum to 80.
All inputs are finite; a program needn't handle non-finite values.
Results may differ from the reference program's by a relative error of at most 0.015.
Values may be sent and summed in bfloat16 or wider, within the bound.
A program may use at most 64 MiB of HBM per device.

```python
import math
import jax
import jax.numpy as jnp
import numpy as np
from jax import lax

D = 512
HEADS = 4
HD = 128
ACTIONS = 16
LAYERS = 2
L = 512
SUB = 32
SD = 16
CENT = 256
BS = 128
NB_G = 16
CAND = 4
GROUPS = 8
USERS = 512
BLOCKS = 128


def set_ends(drawn, rng, least, top_value):
    extent = drawn.shape
    spot = [jax.random.randint(jax.random.fold_in(rng, axis), (), 0, extent[axis]) for axis in range(len(extent))]
    drawn = drawn.at[tuple(spot)].set(least)
    longest = extent.index(max(extent))
    spot[longest] = (spot[longest] + 1) % extent[longest]
    return drawn.at[tuple(spot)].set(top_value)


def steps_of(stream_key, dims, pieces, smallest, largest):
    factor_of, own = 1.0, jax.random.fold_in(stream_key, 6)
    for position, shards_of in pieces:
        steps = jnp.exp(jax.random.uniform(jax.random.fold_in(own, position), (shards_of,), jnp.float32, smallest / len(pieces), largest / len(pieces)))
        factor_of = factor_of * jnp.repeat(steps, dims[position] // shards_of).reshape([-1 if axis == position else 1 for axis in range(len(dims))])
    return factor_of


def length_profile(number_of, total, bound, lean):
    weights = [(1 << 20) // math.isqrt(grade ** lean) + 1 for grade in range(2, number_of + 1)]
    surplus, holding = total - bound - (number_of - 1), [1] * (number_of - 1)
    while surplus > 0:
        movable = [i for i in range(number_of - 1) if holding[i] < bound]
        pool, left = sum([weights[i] for i in movable]), surplus
        for i in movable:
            addition = min(bound - holding[i], max(1, left * weights[i] // pool), surplus)
            holding[i] = holding[i] + addition
            surplus = surplus - addition
    return np.array([bound] + holding)


def uneven(key, number_of, total, reach, skew):
    if number_of == 2:
        one = jax.random.randint(key, (), max(1, total - reach), min(reach, total - 1) + 1)
        return jnp.stack([one, total - one])
    lengths = jnp.asarray(length_profile(number_of, total, reach, skew), jnp.int32)
    twos = (number_of - 1) // 2
    giver, taker = lengths[1:1 + 2 * twos:2], lengths[2:2 + 2 * twos:2]
    slack = jnp.minimum(giver - 1, reach - taker)
    shifted = jax.random.randint(jax.random.fold_in(key, 1), (twos,), 0, 1 << 20) % (slack + 1)
    lengths = lengths.at[1:1 + 2 * twos:2].set(giver - shifted).at[2:2 + 2 * twos:2].set(taker + shifted)
    return lengths[jax.random.permutation(jax.random.fold_in(key, 2), number_of)]


def scatter_about(rng, shape, deviation, limit, pieces=(), held_as=jnp.bfloat16):
    result = deviation * jax.random.normal(rng, shape, jnp.float32)
    if pieces:
        result = result * steps_of(rng, shape, pieces, -0.22, 0.18)
    return jnp.clip(result, -limit, limit).astype(held_as)


def setup_inputs(seed: int = 0) -> dict:
    key_of = jax.random.split(jax.random.key(seed), 11)
    return {
        "history": scatter_about(key_of[0], (USERS, L, D), 1.0, 6.0, ((0, 512),)),
        "actions": set_ends(jax.random.randint(key_of[1], (USERS, L), 0, ACTIONS), jax.random.fold_in(key_of[1], 1), 0, ACTIONS - 1).astype(jnp.int32),
        "action_table": scatter_about(key_of[2], (ACTIONS, D), 0.5, 3.0),
        "w_in": scatter_about(key_of[3], (LAYERS, D, 4 * D), D ** -0.5, 0.25, ((1, 64),)),
        "w_out": scatter_about(key_of[4], (LAYERS, D, D), D ** -0.5, 0.25, ((1, 64),)),
        "w_int": scatter_about(key_of[5], (D, D), D ** -0.5, 0.25, ((0, 64),)),
        "codebook": scatter_about(key_of[6], (SUB, CENT, SD), D ** -0.5, 0.25),
        "codes": set_ends(jax.random.randint(key_of[7], (BLOCKS, BS, SUB), 0, CENT), jax.random.fold_in(key_of[7], 1), 0, CENT - 1).astype(jnp.int32),
        "cand": set_ends(jax.random.randint(key_of[8], (USERS, 4, GROUPS, CAND), 0, NB_G), jax.random.fold_in(key_of[8], 1), 0, NB_G - 1).astype(jnp.int32),
        "counts": jax.vmap(lambda own: uneven(own, 4 * GROUPS, 4 * GROUPS * (CAND + 1) // 2, CAND, 2))(jax.random.split(key_of[9], USERS)).reshape((USERS, 4 * GROUPS)).astype(jnp.int32),
    }


def layer_norm(value):
    mean = lax.optimization_barrier(jnp.mean(value, axis=-1, keepdims=True))
    centred = value - mean
    var = lax.optimization_barrier(jnp.mean(centred * centred, axis=-1, keepdims=True))
    return centred / jnp.sqrt(var + 1e-05)

def reference(history, actions, action_table, w_in, w_out, w_int, codebook, codes, cand, counts):

    def encode(items):
        hist, acts = items
        onehot = (acts[:, None] == jnp.arange(ACTIONS, dtype=jnp.int32)[None, :]).astype(jnp.bfloat16)
        x = hist.astype(jnp.float32) + jnp.dot(onehot, action_table, preferred_element_type=jnp.float32)
        rows = jnp.arange(L, dtype=jnp.int32)
        causal = rows[None, :] <= rows[:, None]
        for layer in range(LAYERS):
            normed = layer_norm(x).astype(jnp.bfloat16)
            proj = jax.nn.silu(jnp.dot(normed, w_in[layer], preferred_element_type=jnp.float32)).astype(jnp.bfloat16)
            u_part = proj[:, 0:D]
            v_part = proj[:, D:2 * D].reshape(L, HEADS, HD).astype(jnp.float32)
            q_part = proj[:, 2 * D:3 * D].reshape(L, HEADS, HD).astype(jnp.float32)
            k_part = proj[:, 3 * D:4 * D].reshape(L, HEADS, HD).astype(jnp.float32)
            logits = jnp.einsum('ihd,jhd->hij', q_part, k_part) / jnp.sqrt(jnp.float32(HD))
            weights = jnp.where(causal[None], jax.nn.silu(logits) / L, 0.0).astype(jnp.bfloat16)
            attn = jnp.einsum('hij,jhd->ihd', weights.astype(jnp.float32), v_part).reshape(L, D)
            gated = (layer_norm(attn) * u_part.astype(jnp.float32)).astype(jnp.bfloat16)
            x = x + jnp.dot(gated, w_out[layer], preferred_element_type=jnp.float32)
        h_rows = layer_norm(x)
        pooled = layer_norm(lax.optimization_barrier(jnp.mean(h_rows.reshape(4, L // 4, D), axis=1))).astype(jnp.bfloat16)
        return jnp.dot(pooled, w_int, preferred_element_type=jnp.float32).astype(jnp.bfloat16)
    interests = lax.map(encode, (history, actions))
    split_int = interests.reshape(USERS, 4, SUB, SD).astype(jnp.float32)
    tables = jnp.einsum('uksj,scj->uksc', split_int, codebook.astype(jnp.float32)).astype(jnp.bfloat16)
    tables = tables.reshape(USERS, 4, SUB * CENT)
    shaped_counts = counts.reshape(USERS, 4, GROUPS)

    def score_user(items):
        tab_user, cand_user, count_user = items
        blocks = jnp.arange(GROUPS, dtype=jnp.int32)[None, :, None] * NB_G + cand_user
        picked = codes[blocks]
        flat = picked + jnp.arange(SUB, dtype=jnp.int32) * CENT
        values = jnp.take_along_axis(tab_user.astype(jnp.float32), flat.reshape(4, -1), axis=1)
        values = lax.optimization_barrier(jnp.sum(values.reshape(4, GROUPS, CAND, BS, SUB), axis=-1))
        live = jnp.arange(CAND, dtype=jnp.int32)[None, None, :] < count_user[:, :, None]
        return jnp.where(live[..., None], values, 0.0)
    return lax.map(score_user, (tables, cand, shaped_counts))
```

```python
import math

import jax
import jax.numpy as jnp
from jax import lax
from jax.experimental import pallas as pl
from jax.experimental.pallas import tpu as pltpu
from jax.sharding import PartitionSpec as P

MESH = pl.DeviceIdType.MESH
F32 = jnp.float32
BF16 = jnp.bfloat16

YS, XL, XH, ZS = 4, 2, 2, 16
XS = XL * XH
ITEMS = YS * XL

D = 512
L = 512
HEADS = 4
HD = 128
ACTIONS = 16
SUB, SD, CENT = 32, 16, 256
NB, BS, CAND, INTR = 16, 128, 4, 4
EPS = 1e-05

IN_BLKS = 16
OUT_BLKS = 4
ALL_BLKS = 2 * IN_BLKS + 3 * OUT_BLKS
Z_OFFS = [8, 7, 9, 6, 10, 5, 11, 4, 12, 3, 13, 2, 14, 1, 15]


def layer_norm(value, eps=EPS):
    mean = jnp.mean(value, axis=-1, keepdims=True)
    centred = value - mean
    var = jnp.mean(centred * centred, axis=-1, keepdims=True)
    return centred * lax.rsqrt(var + eps)


def dot(a, b):
    return lax.dot_general(a, b, (((1,), (0,)), ((), ())), preferred_element_type=F32)


def dot_t(a, b):
    return lax.dot_general(a, b, (((1,), (1,)), ((), ())), preferred_element_type=F32)


def start_values(hist, act, table, x, normed):
    onehot = (
        lax.broadcasted_iota(jnp.int32, (ACTIONS, L), 0) == jnp.broadcast_to(act[...], (ACTIONS, L))
    ).astype(F32)
    rows = 128
    for i in range(L // rows):
        oh = onehot[:, i * rows : (i + 1) * rows].T.astype(BF16)
        part = hist[0, i * rows : (i + 1) * rows].astype(F32) + dot(oh, table[...])
        x[i * rows : (i + 1) * rows] = part
        normed[i * rows : (i + 1) * rows] = layer_norm(part).astype(BF16)


def in_block(weights, layer, blk):
    return weights[layer, blk].reshape(D, 128)


def out_matrix(outs, m):
    return jnp.concatenate([outs[m, j].reshape(D, 128) for j in range(OUT_BLKS)], axis=1)


def project(layer, pair, weights, normed, proj):
    w = jnp.concatenate(
        [in_block(weights, layer, 2 * pair), in_block(weights, layer, 2 * pair + 1)], axis=1
    )
    made = dot(normed[...], w)
    half = 0.5 * made
    made = (half * (1.0 + jnp.tanh(half))).astype(BF16)
    proj[2 * pair] = made[:, :128]
    proj[2 * pair + 1] = made[:, 128:]


def attend(head, proj, attn):
    v, q, k = proj[4 + head], proj[8 + head], proj[12 + head]
    scale = 0.5 / math.sqrt(HD)
    mid = L // 2
    keep = lax.broadcasted_iota(jnp.int32, (mid, mid), 1) <= lax.broadcasted_iota(
        jnp.int32, (mid, mid), 0
    )

    def weigh(qs, ks):
        half = dot_t(qs, ks) * scale
        return 2.0 * half * (0.5 + 0.5 * jnp.tanh(half))

    low = jnp.where(keep, weigh(q[:mid], k[:mid]), 0.0).astype(BF16)
    cross = weigh(q[mid:], k[:mid]).astype(BF16)
    high = jnp.where(keep, weigh(q[mid:], k[mid:]), 0.0).astype(BF16)
    attn[head, :mid] = dot(low, v[:mid])
    attn[head, mid:] = dot(cross, v[:mid]) + dot(high, v[mid:])


def add_out(layer, outs, m, proj, attn, x, normed):
    w = out_matrix(outs, m)
    rows = 128
    for i in range(L // rows):
        r = pl.ds(i * rows, rows)
        a = jnp.concatenate([attn[h, r] for h in range(HEADS)], axis=1)
        u = jnp.concatenate([proj[h, r] for h in range(HEADS)], axis=1)
        gated = (layer_norm(a, EPS * L * L) * u.astype(F32)).astype(BF16)
        new = x[r] + dot(gated, w)
        if layer == 0:
            x[r] = new
            normed[r] = layer_norm(new).astype(BF16)
        else:
            x[r] = layer_norm(new)


def interest_vectors(outs, x):
    per = L // INTR
    rows = [jnp.sum(x[i * per : (i + 1) * per], axis=0, keepdims=True) / per for i in range(INTR)]
    pooled = layer_norm(jnp.concatenate(rows + rows, axis=0))
    pooled = jnp.concatenate([pooled, pooled], axis=0).astype(BF16)
    made = dot(pooled, out_matrix(outs, 2)).astype(BF16).astype(F32)
    return made[: 2 * INTR]


def decode(codes, codebook, cents, decoded):
    eye = (
        lax.broadcasted_iota(jnp.int32, (SD, SD), 0) == lax.broadcasted_iota(jnp.int32, (SD, SD), 1)
    ).astype(BF16)
    for s in range(SUB):
        cents[s] = dot_t(eye, codebook[s])

    @pl.loop(0, NB)
    def _(blk):
        code_t = codes[blk].T
        for s in range(SUB):
            code = jnp.broadcast_to(code_t[s : s + 1], (8, BS))
            spot = code & 127
            made = []
            for part in range(SD // 8):
                r = slice(part * 8, part * 8 + 8)
                low = jnp.take_along_axis(cents[s, r, :128], spot, axis=1)
                high = jnp.take_along_axis(cents[s, r, 128:], spot, axis=1)
                made.append(jnp.where(code < 128, low, high))
            decoded[blk, s * SD : (s + 1) * SD] = jnp.concatenate(made, axis=0).astype(BF16)


def live_slots(cand, counts, mine):
    mine[...] = jnp.zeros_like(mine)
    cnt = jnp.broadcast_to(counts[...], (ITEMS, INTR * ITEMS))
    lane = lax.broadcasted_iota(jnp.int32, (ITEMS, INTR * ITEMS), 1)
    sub = lax.broadcasted_iota(jnp.int32, (ITEMS, INTR * ITEMS), 0)
    slot = lax.broadcasted_iota(jnp.int32, (ITEMS, CAND), 1).astype(F32)
    for k in range(INTR):
        own = jnp.sum(
            jnp.where(lane == k * ITEMS + sub, cnt, 0).astype(F32), axis=1, keepdims=True
        )
        code = jnp.where(slot < own, cand[0, k].astype(F32), -1.0)
        for g in range(ITEMS):
            mine[g, k : k + 1, 0:CAND] = code[g : g + 1]


def kernel(
    hist, act, table, win, wout, wint, codebook, codes, cand, counts,
    out,
    weights, outs, own_rows, got_rows, shard,
    x, normed, proj, attn, cents, decoded,
    slots_mine, slots_got, vec_mine, vec_got, res_mine, res_got,
    ex_s, ex_r, z_s, z_r, p_s, p_r, f_s, f_r, m_s, m_r, i_s, i_r, b_s, b_r,
):
    item, fsdp = lax.axis_index("item"), lax.axis_index("fsdp")
    y, x_lo = item // XL, item % XL
    z, x_hi, c = fsdp // (2 * XH), (fsdp // 2) % XH, fsdp % 2
    zq, zr = z // 4, z % 4
    xx = x_hi * XL + x_lo
    s = c * 2 + x_lo
    partner = (item, fsdp + 1 - 2 * c)

    def z_peer(off):
        return (item, lax.rem(z + off, ZS) * (2 * XH) + x_hi * 2 + c)

    def x_peer(off):
        to = lax.rem(xx + off, XS)
        return (y * XL + to % XL, z * (2 * XH) + (to // XL) * 2 + c)

    def y_peer(off):
        return (lax.rem(y + off, YS) * XL + x_lo, fsdp)

    def item_peer(off):
        return (lax.rem(item + off, ITEMS), fsdp)

    def copy(src, dst, send, recv, to):
        return pltpu.make_async_remote_copy(
            src_ref=src, dst_ref=dst, send_sem=send, recv_sem=recv, device_id=to, device_id_type=MESH
        )

    barrier = pltpu.get_barrier_semaphore()
    met = [partner] + [z_peer(o) for o in range(1, ZS)] + [item_peer(o) for o in range(1, ITEMS)]
    met += [
        (y * XL + lo, z * (2 * XH) + (1 - x_hi) * 2 + c) for lo in range(XL)
    ]
    for peer in met:
        pl.semaphore_signal(barrier, inc=1, device_id=peer, device_id_type=MESH)

    def spread(dst0, ref):
        value = ref.astype(F32)
        for j in range(value.shape[1] // 128):
            own_rows[dst0 + j] = value[:, j * 128 : (j + 1) * 128]

    spread(0, win[0])
    spread(IN_BLKS, win[1])
    spread(2 * IN_BLKS, wout[0])
    spread(2 * IN_BLKS + OUT_BLKS, wout[1])
    spread(2 * IN_BLKS + 2 * OUT_BLKS, wint[...])

    pl.semaphore_wait(barrier, len(met))

    spans = [(0, IN_BLKS), (IN_BLKS, ALL_BLKS)]
    trades = [
        copy(own_rows.at[a:b], got_rows.at[a:b], ex_s.at[i], ex_r.at[i], partner)
        for i, (a, b) in enumerate(spans)
    ]
    for t in trades:
        t.start()

    def assemble(a, b):
        for j in range(a, b):
            mine, theirs = own_rows[j], got_rows[j]
            first = jnp.where(c == 0, mine, theirs)
            second = jnp.where(c == 0, theirs, mine)
            shard[j] = jnp.concatenate([first, second], axis=0).astype(BF16)

    blk = jnp.where(c == 0, y * 2 + x_lo, 8 + x_lo * 4 + y)
    shard_outs = shard.at[2 * IN_BLKS :].reshape(3, OUT_BLKS, 16, 128)

    def z_in(layer, off):
        return copy(
            shard.at[layer * IN_BLKS + blk],
            weights.at[layer, blk, z, x_hi],
            z_s.at[layer, off],
            z_r.at[layer, off],
            z_peer(off),
        )

    def z_out(off):
        return copy(
            shard_outs.at[:, y],
            outs.at[:, y, zq, zr, x_hi],
            z_s.at[2, off],
            z_r.at[2, off],
            z_peer(off),
        )

    def z_out_got(off):
        src = lax.rem(z + ZS - off, ZS)
        ref = outs.at[:, y, src // 4, s, x_hi]
        return copy(ref, ref, z_s.at[2, off], z_r.at[2, off], z_peer(off))

    trades[0].wait_recv()
    assemble(*spans[0])
    for off in Z_OFFS:
        z_in(0, off).start()
    weights[0, blk, z, x_hi] = shard[blk]

    trades[1].wait_recv()
    assemble(*spans[1])

    @pl.when(zr == s)
    def _():
        for off in Z_OFFS:
            z_out(off).start()
        for m in range(3):
            outs[m, y, zq, zr, x_hi] = shard_outs[m, y]

    for off in Z_OFFS:
        z_in(1, off).start()
    weights[1, blk, z, x_hi] = shard[IN_BLKS + blk]

    live_slots(cand, counts, slots_mine)
    slots_got[item] = slots_mine[item]
    slot_copies = [
        copy(
            slots_mine.at[lax.rem(item + o, ITEMS)], slots_got.at[item], m_s.at[o], m_r.at[o], item_peer(o)
        )
        for o in range(1, ITEMS)
    ]
    for t in slot_copies:
        t.start()

    start_values(hist, act, table, x, normed)

    def first_peer(off):
        xp, yp = x_peer(off), y_peer(off)
        return (jnp.where(c == 0, xp[0], yp[0]), jnp.where(c == 0, xp[1], yp[1]))

    def part(chunk):
        if chunk < 2:
            return weights.at[chunk, blk, :, x_hi]
        return outs.at[:, y, :, s, x_hi]

    def step1(chunk, off):
        return copy(part(chunk), part(chunk), p_s.at[chunk, 0, off], p_r.at[chunk, 0, off], first_peer(off))

    def step1_got(chunk, off):
        back_x, back_y = lax.rem(xx + XS - off, XS), lax.rem(y + YS - off, YS)
        lo, hi = back_x % XL, back_x // XL
        f_lo, f_hi = jnp.where(c == 0, lo, x_lo), jnp.where(c == 0, hi, x_hi)
        f_y = jnp.where(c == 0, y, back_y)
        if chunk < 2:
            f_blk = jnp.where(c == 0, f_y * 2 + f_lo, 8 + f_lo * 4 + f_y)
            ref = weights.at[chunk, f_blk, :, f_hi]
        else:
            ref = outs.at[:, f_y, :, c * 2 + f_lo, f_hi]
        return copy(ref, ref, p_s.at[chunk, 0, off], p_r.at[chunk, 0, off], first_peer(off))

    def piece0(chunk, at_y):
        if chunk < 2:
            return weights.at[chunk, pl.ds(at_y * 2, 2)]
        return outs.at[:, at_y, :, 0:2]

    def piece1(chunk, at_x):
        lo, hi = at_x % XL, at_x // XL
        if chunk < 2:
            return weights.at[chunk, pl.ds(8 + lo * 4, 4), :, hi]
        return outs.at[:, :, :, 2 + lo, hi]

    def step2(which, chunk, off, back=False):
        sems = (p_s.at[chunk, 1, off], p_r.at[chunk, 1, off])
        at_y = lax.rem(y + YS - off, YS) if back else y
        at_x = lax.rem(xx + XS - off, XS) if back else xx
        if which == 0:
            return copy(piece0(chunk, at_y), piece0(chunk, at_y), *sems, y_peer(off))
        return copy(piece1(chunk, at_x), piece1(chunk, at_x), *sems, x_peer(off))

    def forward(which, chunk, off):
        sems = (f_s.at[chunk, off], f_r.at[chunk, off])
        at_y, at_x = lax.rem(y + YS - off, YS), lax.rem(xx + XS - off, XS)
        if which == 0:
            return copy(piece0(chunk, at_y), piece0(chunk, at_y), *sems, partner)
        return copy(piece1(chunk, at_x), piece1(chunk, at_x), *sems, partner)

    def after_z(chunk):
        if chunk < 2:
            for off in Z_OFFS:
                z_in(chunk, off).wait_recv()
        else:
            for off in Z_OFFS:
                src = lax.rem(z + ZS - off, ZS)
                pl.when(src % 4 == s)(lambda off=off: z_out_got(off).wait_recv())
        for off in (2, 1, 3):
            step1(chunk, off).start()

    def after_step1(chunk):
        for off in (1, 2, 3):
            step1_got(chunk, off).wait_recv()

        def go(which):
            for off in (2, 1, 3):
                step2(which, chunk, off).start()
            forward(which, chunk, 0).start()

        pl.when(c == 0)(lambda: go(0))
        pl.when(c == 1)(lambda: go(1))

    def after_step2(chunk):
        def go(which):
            for off in (1, 3, 2):
                step2(which, chunk, off, back=True).wait_recv()
                forward(which, chunk, off).start()

        pl.when(c == 0)(lambda: go(0))
        pl.when(c == 1)(lambda: go(1))

    def after_forward(chunk):
        def go(which):
            for off in (0, 1, 3, 2):
                forward(which, chunk, off).wait_recv()

        pl.when(c == 0)(lambda: go(1))
        pl.when(c == 1)(lambda: go(0))

    after_z(0)
    after_z(2)
    after_z(1)
    after_step1(0)
    after_step1(2)
    after_step1(1)

    decode(codes, codebook, cents, decoded)

    after_step2(0)
    after_forward(0)
    for pair in range(8):
        project(0, pair, weights, normed, proj)
    after_step2(2)
    for head in range(HEADS):
        attend(head, proj, attn)
    after_forward(2)
    add_out(0, outs, 0, proj, attn, x, normed)
    after_step2(1)
    after_forward(1)
    for pair in range(8):
        project(1, pair, weights, normed, proj)
    for head in range(HEADS):
        attend(head, proj, attn)
    add_out(1, outs, 1, proj, attn, x, normed)

    vec = interest_vectors(outs, x)
    vec_mine[...] = vec
    vec_copies = [
        copy(vec_mine, vec_got.at[item], i_s.at[o], i_r.at[o], item_peer(o)) for o in range(1, ITEMS)
    ]
    for t in vec_copies:
        t.start()
    vec_got[item] = vec

    def got_from(off):
        return lax.rem(item + ITEMS - off, ITEMS)

    for o in range(1, ITEMS):
        ref = slots_got.at[got_from(o)]
        copy(ref, ref, m_s.at[o], m_r.at[o], item_peer(o)).wait_recv()
    for o in range(1, ITEMS):
        ref = vec_got.at[got_from(o)]
        copy(ref, ref, i_s.at[o], i_r.at[o], item_peer(o)).wait_recv()

    all_vec = vec_got[...].reshape(ITEMS * 8, D).astype(BF16)
    chosen = [[jnp.zeros((8, BS), F32) for _ in range(CAND)] for _ in range(ITEMS)]
    wanted = [
        [jnp.broadcast_to(slots_got[u, :, b : b + 1], (8, BS)) for b in range(CAND)]
        for u in range(ITEMS)
    ]
    for nb in range(NB):
        scored = dot(all_vec, decoded[nb])
        for u in range(ITEMS):
            mine = scored[u * 8 : u * 8 + 8]
            for b in range(CAND):
                chosen[u][b] = jnp.where(wanted[u][b] == float(nb), mine, chosen[u][b])
    for u in range(ITEMS):
        for h in range(CAND // 2):
            res_mine[u, h] = jnp.concatenate(
                [chosen[u][2 * h][:INTR], chosen[u][2 * h + 1][:INTR]], axis=0
            )

    res_copies = [
        copy(
            res_mine.at[lax.rem(item + o, ITEMS)], res_got.at[item], b_s.at[o], b_r.at[o], item_peer(o)
        )
        for o in range(1, ITEMS)
    ]
    for t in res_copies:
        t.start()
    res_got[item] = res_mine[item]

    for t in trades + slot_copies + vec_copies:
        t.wait_send()
    for layer in range(2):
        for off in Z_OFFS:
            z_in(layer, off).wait_send()

    @pl.when(zr == s)
    def _():
        for off in Z_OFFS:
            z_out(off).wait_send()

    for chunk in range(3):
        for off in (1, 2, 3):
            step1(chunk, off).wait_send()

        def go(which, chunk=chunk):
            for off in (1, 2, 3):
                step2(which, chunk, off).wait_send()
            for off in (0, 1, 2, 3):
                forward(which, chunk, off).wait_send()

        pl.when(c == 0)(lambda: go(0))
        pl.when(c == 1)(lambda: go(1))
    for o in range(1, ITEMS):
        ref = res_got.at[got_from(o)]
        copy(ref, ref, b_s.at[o], b_r.at[o], item_peer(o)).wait_recv()
    for t in res_copies:
        t.wait_send()
    out[...] = res_got[...]


def body(history, actions, action_table, w_in, w_out, w_int, codebook, codes, cand, counts):
    vmem = pl.BlockSpec(memory_space=pltpu.VMEM)
    dma = pltpu.SemaphoreType.DMA
    made = pl.pallas_call(
        kernel,
        out_shape=jax.ShapeDtypeStruct((ITEMS, CAND // 2, 2 * INTR, BS), F32),
        in_specs=[vmem] * 10,
        out_specs=vmem,
        scratch_shapes=[
            pltpu.VMEM((2, IN_BLKS, ZS, XH, 16, 128), BF16),
            pltpu.VMEM((3, OUT_BLKS, 4, 4, XH, 16, 128), BF16),
            pltpu.VMEM((ALL_BLKS, 8, 128), F32),
            pltpu.VMEM((ALL_BLKS, 8, 128), F32),
            pltpu.VMEM((ALL_BLKS, 16, 128), BF16),
            pltpu.VMEM((L, D), F32),
            pltpu.VMEM((L, D), BF16),
            pltpu.VMEM((IN_BLKS, L, 128), BF16),
            pltpu.VMEM((HEADS, L, HD), F32),
            pltpu.VMEM((SUB, SD, CENT), F32),
            pltpu.VMEM((NB, D, BS), BF16),
            pltpu.VMEM((ITEMS, 8, 128), F32),
            pltpu.VMEM((ITEMS, 8, 128), F32),
            pltpu.VMEM((8, D), F32),
            pltpu.VMEM((ITEMS, 8, D), F32),
            pltpu.VMEM((ITEMS, CAND // 2, 2 * INTR, BS), F32),
            pltpu.VMEM((ITEMS, CAND // 2, 2 * INTR, BS), F32),
            dma((2,)),
            dma((2,)),
            dma((3, ZS)),
            dma((3, ZS)),
            dma((3, 2, 4)),
            dma((3, 2, 4)),
            dma((3, 4)),
            dma((3, 4)),
            dma((ITEMS,)),
            dma((ITEMS,)),
            dma((ITEMS,)),
            dma((ITEMS,)),
            dma((ITEMS,)),
            dma((ITEMS,)),
        ],
        compiler_params=pltpu.CompilerParams(
            collective_id=0, has_side_effects=True, vmem_limit_bytes=48 * 1024 * 1024
        ),
        name="encode_and_score",
    )(history, actions, action_table, w_in, w_out, w_int, codebook, codes, cand, counts)
    made = made.reshape(ITEMS, CAND, INTR, BS)
    return jnp.transpose(made, (2, 0, 1, 3))[None]


def solution(mesh):
    placed = (
        P(("item", "fsdp"), None, None),
        P(("item", "fsdp"), None),
        P(),
        P(None, "fsdp", None),
        P(None, "fsdp", None),
        P("fsdp", None),
        P(),
        P("item", None, None),
        P(("item", "fsdp"), None, None, None),
        P(("item", "fsdp"), None),
    )
    return jax.shard_map(
        body,
        mesh=mesh,
        in_specs=placed,
        out_specs=P(("item", "fsdp"), None, None, None, None),
        check_vma=False,
    )
```

```python
import math

import jax
import jax.numpy as jnp
from jax import lax
from jax.experimental import pallas as pl
from jax.experimental.pallas import tpu as pltpu
from jax.sharding import PartitionSpec as P

MESH = pl.DeviceIdType.MESH
F32 = jnp.float32
BF16 = jnp.bfloat16

YS, XL, XH, ZS = 4, 2, 2, 16
XS = XL * XH
ITEMS = YS * XL

D = 512
L = 512
HEADS = 4
HD = 128
ACTIONS = 16
SUB, SD, CENT = 32, 16, 256
NB, BS, CAND, INTR = 16, 128, 4, 4
EPS = 1e-05

IN_BLKS = 16
OUT_BLKS = 4
ALL_BLKS = 2 * IN_BLKS + 3 * OUT_BLKS
ZH = ZS // 2
ORDER = (0, 2, 1)


def layer_norm(value, eps=EPS):
    mean = jnp.mean(value, axis=-1, keepdims=True)
    centred = value - mean
    var = jnp.mean(centred * centred, axis=-1, keepdims=True)
    return centred * lax.rsqrt(var + eps)


def dot(a, b):
    return lax.dot_general(a, b, (((1,), (0,)), ((), ())), preferred_element_type=F32)


def dot_t(a, b):
    return lax.dot_general(a, b, (((1,), (1,)), ((), ())), preferred_element_type=F32)


def start_values(hist, act, table, x, normed):
    onehot = (
        lax.broadcasted_iota(jnp.int32, (ACTIONS, L), 0) == jnp.broadcast_to(act[...], (ACTIONS, L))
    ).astype(F32)
    rows = 128
    for i in range(L // rows):
        oh = onehot[:, i * rows : (i + 1) * rows].T.astype(BF16)
        part = hist[0, i * rows : (i + 1) * rows].astype(F32) + dot(oh, table[...])
        x[i * rows : (i + 1) * rows] = part
        normed[i * rows : (i + 1) * rows] = layer_norm(part).astype(BF16)


def in_block(weights, layer, blk):
    return weights[layer, blk].reshape(D, 128)


def out_matrix(outs, m):
    return jnp.concatenate([outs[m, j].reshape(D, 128) for j in range(OUT_BLKS)], axis=1)


def project(layer, pair, weights, normed, proj):
    w = jnp.concatenate(
        [in_block(weights, layer, 2 * pair), in_block(weights, layer, 2 * pair + 1)], axis=1
    )
    made = dot(normed[...], w)
    half = 0.5 * made
    made = (half * (1.0 + jnp.tanh(half))).astype(BF16)
    proj[2 * pair] = made[:, :128]
    proj[2 * pair + 1] = made[:, 128:]


def attend(head, proj, attn):
    v, q, k = proj[4 + head], proj[8 + head], proj[12 + head]
    scale = 0.5 / math.sqrt(HD)
    mid = L // 2
    keep = lax.broadcasted_iota(jnp.int32, (mid, mid), 1) <= lax.broadcasted_iota(
        jnp.int32, (mid, mid), 0
    )

    def weigh(qs, ks):
        half = dot_t(qs, ks) * scale
        return 2.0 * half * (0.5 + 0.5 * jnp.tanh(half))

    low = jnp.where(keep, weigh(q[:mid], k[:mid]), 0.0).astype(BF16)
    cross = weigh(q[mid:], k[:mid]).astype(BF16)
    high = jnp.where(keep, weigh(q[mid:], k[mid:]), 0.0).astype(BF16)
    attn[head, :mid] = dot(low, v[:mid])
    attn[head, mid:] = dot(cross, v[:mid]) + dot(high, v[mid:])


def add_out(layer, outs, m, proj, attn, x, normed):
    w = out_matrix(outs, m)
    rows = 128
    for i in range(L // rows):
        r = pl.ds(i * rows, rows)
        a = jnp.concatenate([attn[h, r] for h in range(HEADS)], axis=1)
        u = jnp.concatenate([proj[h, r] for h in range(HEADS)], axis=1)
        gated = (layer_norm(a, EPS * L * L) * u.astype(F32)).astype(BF16)
        new = x[r] + dot(gated, w)
        if layer == 0:
            x[r] = new
            normed[r] = layer_norm(new).astype(BF16)
        else:
            x[r] = layer_norm(new)


def interest_vectors(outs, x):
    per = L // INTR
    rows = [jnp.sum(x[i * per : (i + 1) * per], axis=0, keepdims=True) / per for i in range(INTR)]
    pooled = layer_norm(jnp.concatenate([r for r in rows for _ in range(CAND)], axis=0))
    return dot(pooled.astype(BF16), out_matrix(outs, 2)).astype(BF16)


def decode(first, last, codes, codebook, cents, decoded):
    if first == 0:
        for s in range(SUB):
            cents[s] = codebook[s].astype(F32)

    @pl.loop(first, last)
    def _(blk):
        for s in range(SUB):
            code = jnp.broadcast_to(codes[blk, s : s + 1], (8, BS))
            spot = code & 127
            made = []
            for part in range(SD // 8):
                r = slice(part * 8, part * 8 + 8)
                low = jnp.take_along_axis(cents[s, r, :128], spot, axis=1)
                high = jnp.take_along_axis(cents[s, r, 128:], spot, axis=1)
                made.append(jnp.where(code < 128, low, high))
            decoded[blk, s * SD : (s + 1) * SD] = jnp.concatenate(made, axis=0).astype(BF16)


def live_slots(cand, counts, mine):
    mine[...] = jnp.zeros_like(mine)
    cnt = jnp.broadcast_to(counts[...].astype(F32), (CAND, INTR * ITEMS))
    slot = lax.broadcasted_iota(jnp.int32, (CAND, ITEMS), 0).astype(F32)
    rows = []
    for k in range(INTR):
        own = cnt[:, k * ITEMS : (k + 1) * ITEMS]
        rows.append(jnp.where(slot < own, cand[0, k].astype(F32), -1.0))
    mine[:, :ITEMS] = jnp.concatenate(rows, axis=0)


def kernel(
    hist_h, act_h, table_h, win_h, wout_h, wint_h, codebook_h, codes_h, cand_h, counts_h,
    out,
    hist, act, table, win, wout, wint, codebook, codes, cand, counts,
    weights, outs, own_rows, got_rows, shard,
    x, normed, proj, attn, cents, decoded,
    slots_mine, slots_got, wanted, vec_mine, vec_got, res_mine, res_got,
    in_sem, late_sem,
    ex_s, ex_r, z_s, z_r, p1_s, p1_r, p2_s, p2_r, p3_s, f_s, f_r, m_s, m_r, i_s, i_r, b_s, b_r,
):
    item, fsdp = lax.axis_index("item"), lax.axis_index("fsdp")
    y, x_lo = item // XL, item % XL
    z, x_hi, c = fsdp // (2 * XH), (fsdp // 2) % XH, fsdp % 2
    zq, zr = z // 4, z % 4
    half = z // ZH
    xx = x_hi * XL + x_lo
    s = c * 2 + x_lo
    partner = (item, fsdp + 1 - 2 * c)

    def at_z(to):
        return (item, to * (2 * XH) + x_hi * 2 + c)

    def x_peer(off):
        to = lax.rem(xx + off, XS)
        return (y * XL + to % XL, z * (2 * XH) + (to // XL) * 2 + c)

    def y_peer(off):
        return (lax.rem(y + off, YS) * XL + x_lo, fsdp)

    def item_peer(off):
        return (lax.rem(item + off, ITEMS), fsdp)

    def copy(src, dst, send, recv, to):
        return pltpu.make_async_remote_copy(
            src_ref=src, dst_ref=dst, send_sem=send, recv_sem=recv, device_id=to, device_id_type=MESH
        )

    barrier = pltpu.get_barrier_semaphore()
    near = [partner] + [item_peer(o) for o in range(1, ITEMS)]
    near += [(y * XL + lo, z * (2 * XH) + (1 - x_hi) * 2 + c) for lo in range(XL)]
    own_half = [at_z(half * ZH + lax.rem(z + o, ZH)) for o in range(1, ZH)]

    def greet(sem, peers):
        for peer in peers:
            pl.semaphore_signal(sem, inc=1, device_id=peer, device_id_type=MESH)

    operands = [
        (win_h, win), (wout_h, wout), (wint_h, wint), (hist_h, hist), (act_h, act), (table_h, table),
        (codebook_h, codebook), (codes_h, codes), (cand_h, cand), (counts_h, counts),
    ]
    fetches = [pltpu.make_async_copy(h, v, in_sem.at[i]) for i, (h, v) in enumerate(operands)]
    for t in fetches[:3]:
        t.start()
    greet(barrier, near + own_half)

    @pl.when(half == 0)
    def _():
        greet(barrier, [at_z(ZH + t) for t in range(ZH)])

    for t in fetches[3:]:
        t.start()

    def spread(dst0, value):
        value = value.astype(F32)
        for j in range(value.shape[1] // 128):
            own_rows[dst0 + j] = value[:, j * 128 : (j + 1) * 128]

    fetches[0].wait()
    spread(0, win[0])

    def prepare(last):
        for t in fetches[3:]:
            t.wait()
        live_slots(cand, counts, slots_mine)
        start_values(hist, act, table, x, normed)
        decode(0, last, codes, codebook, cents, decoded)

    pl.when(zq == 0)(lambda: prepare(NB))

    @pl.when(half == 0)
    def _():
        pl.semaphore_wait(barrier, len(near) + ZH - 1)

    @pl.when(half == 1)
    def _():
        pl.semaphore_wait(barrier, len(near) + ZS - 1)

    spans = [(0, IN_BLKS), (IN_BLKS, ALL_BLKS)]
    trades = [
        copy(own_rows.at[a:b], got_rows.at[a:b], ex_s.at[i], ex_r.at[i], partner)
        for i, (a, b) in enumerate(spans)
    ]
    trades[0].start()

    @pl.when(half == 1)
    def _():
        greet(late_sem, [at_z(t) for t in range(ZH)])

    spread(IN_BLKS, win[1])
    fetches[1].wait()
    spread(2 * IN_BLKS, wout[0])
    spread(2 * IN_BLKS + OUT_BLKS, wout[1])
    fetches[2].wait()
    spread(2 * IN_BLKS + 2 * OUT_BLKS, wint[...])
    trades[1].start()

    def assemble(a, b):
        for j in range(a, b):
            mine, theirs = own_rows[j], got_rows[j]
            first = jnp.where(c == 0, mine, theirs)
            second = jnp.where(c == 0, theirs, mine)
            shard[j] = jnp.concatenate([first, second], axis=0).astype(BF16)

    blk = jnp.where(c == 0, y * 2 + x_lo, 8 + x_lo * 4 + y)
    shard_outs = shard.at[2 * IN_BLKS :].reshape(3, OUT_BLKS, 16, 128)

    def z_ends(chunk):
        if chunk < 2:
            return shard.at[chunk * IN_BLKS + blk], weights.at[chunk, blk, z, x_hi]
        return shard_outs.at[:, y], outs.at[:, y, zq, zr, x_hi]

    def z_send(chunk, to):
        copy(*z_ends(chunk), z_s.at[chunk], z_r.at[chunk, half], at_z(to)).start()

    def z_keep(chunk):
        src, dst = z_ends(chunk)
        pltpu.make_async_copy(src, dst, z_r.at[chunk, half]).start()

    def if_has(chunk, act):
        if chunk < 2:
            act()
        else:
            pl.when(zr == s)(act)

    def z_near(chunk):
        def act():
            @pl.when(half == 1)
            def _():
                for t in range(ZH):
                    z_send(chunk, t)

            z_keep(chunk)
            for t in range(ZH - 1):
                z_send(chunk, half * ZH + t + jnp.where(t >= z % ZH, 1, 0))

        if_has(chunk, act)

    def z_far(chunk):
        def act():
            for t in range(ZH):
                z_send(chunk, ZH + t)

        if_has(chunk, act)

    def group(chunk, n_in, n_out):
        if chunk < 2:
            return weights.reshape(2 * IN_BLKS * ZS * XH, 16, 128).at[:n_in]
        return outs.reshape(3 * OUT_BLKS * ZS * XH, 16, 128).at[:n_out]

    trades[0].wait_recv()
    assemble(*spans[0])
    z_near(0)
    trades[1].wait_recv()
    assemble(*spans[1])
    z_near(2)
    z_near(1)

    pl.when(zq > 0)(lambda: prepare(NB // 2))

    slots_got[item] = slots_mine[...]
    slot_copies = [
        copy(slots_mine, slots_got.at[item], m_s.at[o], m_r.at[o], item_peer(o))
        for o in range(1, ITEMS)
    ]
    for t in slot_copies:
        t.start()

    def first_peer(off):
        xp, yp = x_peer(off), y_peer(off)
        return (jnp.where(c == 0, xp[0], yp[0]), jnp.where(c == 0, xp[1], yp[1]))

    def part(chunk, h):
        if chunk < 2:
            return weights.at[chunk, blk, pl.ds(h * ZH, ZH), x_hi]
        return outs.at[:, y, pl.ds(h * 2, 2), s, x_hi]

    def piece(which, chunk, h, off):
        if which == 0:
            at_y = lax.rem(y + YS - off, YS)
            if chunk < 2:
                return weights.at[chunk, pl.ds(at_y * 2, 2), pl.ds(h * ZH, ZH)]
            return outs.at[:, at_y, pl.ds(h * 2, 2), 0:2]
        at_x = lax.rem(xx + XS - off, XS)
        lo, hi = at_x % XL, at_x // XL
        if chunk < 2:
            return weights.at[chunk, pl.ds(8 + lo * 4, 4), pl.ds(h * ZH, ZH), hi]
        return outs.at[:, :, pl.ds(h * 2, 2), 2 + lo, hi]

    def piece_part(which, chunk, h, off, n):
        ref = piece(which, chunk, h, off)
        if chunk < 2:
            count = 1 if which == 0 else 2
            return ref.at[n * count : (n + 1) * count]
        return ref.at[:, n] if which == 0 else ref.at[:, :, n]

    def core_half(which, chunk, h):
        if chunk < 2:
            return weights.at[chunk, which * 8 : which * 8 + 8, pl.ds(h * ZH, ZH)]
        return outs.at[:, :, pl.ds(h * 2, 2), which * 2 : which * 2 + 2]

    def by_core(act):
        pl.when(c == 0)(lambda: act(0))
        pl.when(c == 1)(lambda: act(1))

    def after_z(chunk, h):
        ref = part(chunk, h)
        copy(ref, ref, z_s.at[chunk], z_r.at[chunk, h], partner).wait_recv()
        for off in (2, 1, 3):
            copy(ref, ref, p1_s.at[chunk, h], p1_r.at[chunk, h], first_peer(off)).start()

    def after_step1(chunk, h):
        ref = group(chunk, 3 * ZH, 3 * 6)
        copy(ref, ref, p1_s.at[chunk, h], p1_r.at[chunk, h], partner).wait_recv()

        def act(which):
            ref = piece(which, chunk, h, 0)
            peer = y_peer if which == 0 else x_peer
            for off in (1, 3):
                copy(ref, ref, p2_s.at[chunk, h], p2_r.at[chunk, h, off], peer(off)).start()
            copy(ref, ref, f_s.at[chunk, h], f_r.at[chunk, h], partner).start()

        by_core(act)

    def after_near(chunk, h):
        def act(which):
            peer = y_peer if which == 0 else x_peer
            for off in (1, 3):
                ref = piece(which, chunk, h, off)
                copy(ref, ref, p2_s.at[chunk, h], p2_r.at[chunk, h, off], partner).wait_recv()
                on = piece_part(which, chunk, h, off, off // 2)
                copy(on, on, p3_s.at[chunk, h], p2_r.at[chunk, h, 2], peer(off)).start()
                copy(ref, ref, f_s.at[chunk, h], f_r.at[chunk, h], partner).start()

        by_core(act)

    def after_ring(chunk, h):
        def act(which):
            ref = piece(which, chunk, h, 2)
            copy(ref, ref, p3_s.at[chunk, h], p2_r.at[chunk, h, 2], partner).wait_recv()
            copy(ref, ref, f_s.at[chunk, h], f_r.at[chunk, h], partner).start()

        by_core(act)

    def after_forward(chunk, h):
        def act(which):
            ref = core_half(1 - which, chunk, h)
            copy(ref, ref, f_s.at[chunk, h], f_r.at[chunk, h], partner).wait_recv()

        by_core(act)

    own, other = half, 1 - half
    for chunk in ORDER:
        after_z(chunk, own)

    @pl.when(half == 0)
    def _():
        pl.semaphore_wait(late_sem, ZH)
        for chunk in ORDER:
            z_far(chunk)

    for chunk in ORDER:
        after_step1(chunk, own)
    for chunk in ORDER:
        after_z(chunk, other)
    for chunk in ORDER:
        after_near(chunk, own)
    for chunk in ORDER:
        after_step1(chunk, other)
    pl.when(zq > 0)(lambda: decode(NB // 2, NB, codes, codebook, cents, decoded))
    for chunk in ORDER:
        after_ring(chunk, own)

    def got_from(off):
        return lax.rem(item + ITEMS - off, ITEMS)

    for o in range(1, ITEMS):
        ref = slots_got.at[got_from(o)]
        copy(ref, ref, m_s.at[o], m_r.at[o], item_peer(o)).wait_recv()
    rows = ITEMS * INTR * CAND
    lane = lax.broadcasted_iota(jnp.int32, (rows, 128), 1)
    picked = jnp.where(lane == item, slots_got[...].reshape(rows, 128), 0.0)
    wanted[...] = jnp.broadcast_to(jnp.sum(picked, axis=1, keepdims=True), (rows, 128))

    for chunk in ORDER:
        after_near(chunk, other)
    after_ring(0, other)
    after_forward(0, own)
    after_forward(0, other)
    for pair in range(8):
        project(0, pair, weights, normed, proj)
    after_ring(2, other)
    for head in range(HEADS):
        attend(head, proj, attn)
    after_ring(1, other)
    after_forward(2, own)
    after_forward(2, other)
    add_out(0, outs, 0, proj, attn, x, normed)
    after_forward(1, own)
    after_forward(1, other)
    for pair in range(8):
        project(1, pair, weights, normed, proj)
    for head in range(HEADS):
        attend(head, proj, attn)
    add_out(1, outs, 1, proj, attn, x, normed)

    vec = interest_vectors(outs, x)
    vec_mine[...] = vec
    vec_copies = [
        copy(vec_mine, vec_got.at[item], i_s.at[o], i_r.at[o], item_peer(o)) for o in range(1, ITEMS)
    ]
    for t in vec_copies:
        t.start()
    vec_got[item] = vec

    for t in trades + slot_copies:
        t.wait_send()
    for chunk in range(3):

        def sent(chunk=chunk):
            ref = group(chunk, ZS - 1, 3 * (ZS - 1))
            copy(ref, ref, z_s.at[chunk], z_r.at[chunk, 0], partner).wait_send()

        if_has(chunk, sent)
        for h in range(2):
            ref = group(chunk, 3 * ZH, 3 * 6)
            copy(ref, ref, p1_s.at[chunk, h], p1_r.at[chunk, h], partner).wait_send()
            ref = group(chunk, 2 * 4 * ZH, 2 * 24)
            copy(ref, ref, p2_s.at[chunk, h], p2_r.at[chunk, h, 0], partner).wait_send()
            ref = group(chunk, 4 * ZH, 24)
            copy(ref, ref, p3_s.at[chunk, h], p2_r.at[chunk, h, 0], partner).wait_send()
            ref = core_half(0, chunk, h)
            copy(ref, ref, f_s.at[chunk, h], f_r.at[chunk, h], partner).wait_send()

    for o in range(1, ITEMS):
        ref = vec_got.at[got_from(o)]
        copy(ref, ref, i_s.at[o], i_r.at[o], item_peer(o)).wait_recv()

    all_vec = vec_got[...].reshape(rows, D)
    chosen = jnp.zeros((rows, BS), F32)
    for pair in range(NB // 2):
        items = jnp.concatenate([decoded[2 * pair], decoded[2 * pair + 1]], axis=1)
        scored = dot(all_vec, items)
        want = wanted[...]
        chosen = jnp.where(want == float(2 * pair), scored[:, :BS], chosen)
        chosen = jnp.where(want == float(2 * pair + 1), scored[:, BS:], chosen)
    res_mine[...] = chosen.reshape(ITEMS, INTR * CAND, BS)

    res_copies = [
        copy(
            res_mine.at[lax.rem(item + o, ITEMS)], res_got.at[item], b_s.at[o], b_r.at[o], item_peer(o)
        )
        for o in range(1, ITEMS)
    ]
    for t in res_copies:
        t.start()
    res_got[item] = res_mine[item]
    for t in vec_copies:
        t.wait_send()
    for o in range(1, ITEMS):
        ref = res_got.at[got_from(o)]
        copy(ref, ref, b_s.at[o], b_r.at[o], item_peer(o)).wait_recv()
    for t in res_copies:
        t.wait_send()
    out[...] = res_got[...]


def body(history, actions, action_table, w_in, w_out, w_int, codebook, codes, cand, counts):
    hbm = pl.BlockSpec(memory_space=pl.ANY)
    dma = pltpu.SemaphoreType.DMA
    operands = (
        history, actions, action_table, w_in, w_out, w_int,
        jnp.transpose(codebook, (0, 2, 1)),
        jnp.transpose(codes, (0, 2, 1)),
        jnp.transpose(cand, (0, 1, 3, 2)),
        counts,
    )
    made = pl.pallas_call(
        kernel,
        out_shape=jax.ShapeDtypeStruct((ITEMS, INTR * CAND, BS), F32),
        in_specs=[hbm] * 10,
        out_specs=pl.BlockSpec(memory_space=pltpu.VMEM),
        scratch_shapes=[pltpu.VMEM(a.shape, a.dtype) for a in operands]
        + [
            pltpu.VMEM((2, IN_BLKS, ZS, XH, 16, 128), BF16),
            pltpu.VMEM((3, OUT_BLKS, 4, 4, XH, 16, 128), BF16),
            pltpu.VMEM((ALL_BLKS, 8, 128), F32),
            pltpu.VMEM((ALL_BLKS, 8, 128), F32),
            pltpu.VMEM((ALL_BLKS, 16, 128), BF16),
            pltpu.VMEM((L, D), F32),
            pltpu.VMEM((L, D), BF16),
            pltpu.VMEM((IN_BLKS, L, 128), BF16),
            pltpu.VMEM((HEADS, L, HD), F32),
            pltpu.VMEM((SUB, SD, CENT), F32),
            pltpu.VMEM((NB, D, BS), BF16),
            pltpu.VMEM((INTR * CAND, 128), F32),
            pltpu.VMEM((ITEMS, INTR * CAND, 128), F32),
            pltpu.VMEM((ITEMS * INTR * CAND, 128), F32),
            pltpu.VMEM((INTR * CAND, D), BF16),
            pltpu.VMEM((ITEMS, INTR * CAND, D), BF16),
            pltpu.VMEM((ITEMS, INTR * CAND, BS), F32),
            pltpu.VMEM((ITEMS, INTR * CAND, BS), F32),
            dma((len(operands),)),
            pltpu.SemaphoreType.REGULAR,
            dma((2,)),
            dma((2,)),
            dma((3,)),
            dma((3, 2)),
            dma((3, 2)),
            dma((3, 2)),
            dma((3, 2)),
            dma((3, 2, 4)),
            dma((3, 2)),
            dma((3, 2)),
            dma((3, 2)),
            dma((ITEMS,)),
            dma((ITEMS,)),
            dma((ITEMS,)),
            dma((ITEMS,)),
            dma((ITEMS,)),
            dma((ITEMS,)),
        ],
        compiler_params=pltpu.CompilerParams(
            collective_id=0, has_side_effects=True, vmem_limit_bytes=56 * 1024 * 1024
        ),
        name="encode_and_score",
    )(*operands)
    made = made.reshape(ITEMS, INTR, CAND, BS)
    return jnp.transpose(made, (1, 0, 2, 3))[None]


def solution(mesh):
    placed = (
        P(("item", "fsdp"), None, None),
        P(("item", "fsdp"), None),
        P(),
        P(None, "fsdp", None),
        P(None, "fsdp", None),
        P("fsdp", None),
        P(),
        P("item", None, None),
        P(("item", "fsdp"), None, None, None),
        P(("item", "fsdp"), None),
    )
    return jax.shard_map(
        body,
        mesh=mesh,
        in_specs=placed,
        out_specs=P(("item", "fsdp"), None, None, None, None),
        check_vma=False,
    )
```

```python
import functools
import math

import jax
import jax.numpy as jnp
from jax import lax
from jax.experimental import pallas as pl
from jax.experimental.pallas import tpu as pltpu
from jax.sharding import PartitionSpec as P

MESH = pl.DeviceIdType.MESH
F32 = jnp.float32
BF16 = jnp.bfloat16

YS, XL, XH, ZS = 4, 2, 2, 16
XS = XL * XH
ITEMS = YS * XL

D = 512
L = 512
HEADS = 4
HD = 128
ACTIONS = 16
SUB, SD, CENT = 32, 16, 256
NB, BS, CAND, INTR = 16, 128, 4, 4
EPS = 1e-05

IN_BLKS = 16
OUT_BLKS = 4
ALL_BLKS = 2 * IN_BLKS + 3 * OUT_BLKS
ZP = 4
IN0, IN1, OUT0, OUT1 = range(4)
ORDER = (IN0, OUT0, IN1, OUT1)
OUT_PART = {OUT0: (0, 1), OUT1: (1, 3)}


def layer_norm(value, eps=EPS):
    mean = jnp.mean(value, axis=-1, keepdims=True)
    centred = value - mean
    var = jnp.mean(centred * centred, axis=-1, keepdims=True)
    return centred * lax.rsqrt(var + eps)


def dot(a, b):
    return lax.dot_general(a, b, (((1,), (0,)), ((), ())), preferred_element_type=F32)


def dot_t(a, b):
    return lax.dot_general(a, b, (((1,), (1,)), ((), ())), preferred_element_type=F32)


def start_values(hist, act, table, x, normed):
    onehot = (
        lax.broadcasted_iota(jnp.int32, (ACTIONS, L), 0) == jnp.broadcast_to(act[...], (ACTIONS, L))
    ).astype(F32)
    rows = 128
    for i in range(L // rows):
        oh = onehot[:, i * rows : (i + 1) * rows].T.astype(BF16)
        part = hist[0, i * rows : (i + 1) * rows].astype(F32) + dot(oh, table[...])
        x[i * rows : (i + 1) * rows] = part
        normed[i * rows : (i + 1) * rows] = layer_norm(part).astype(BF16)


def in_block(weights, layer, blk):
    return weights[layer, blk].reshape(D, 128)


def out_matrix(outs, m):
    return jnp.concatenate([outs[m, j].reshape(D, 128) for j in range(OUT_BLKS)], axis=1)


def project(layer, pair, weights, normed, proj):
    w = jnp.concatenate(
        [in_block(weights, layer, 2 * pair), in_block(weights, layer, 2 * pair + 1)], axis=1
    )
    made = dot(normed[...], w)
    half = 0.5 * made
    made = (half * (1.0 + jnp.tanh(half))).astype(BF16)
    proj[2 * pair] = made[:, :128]
    proj[2 * pair + 1] = made[:, 128:]


def attend(head, proj, attn):
    v, q, k = proj[4 + head], proj[8 + head], proj[12 + head]
    scale = 0.5 / math.sqrt(HD)
    mid = L // 2
    keep = lax.broadcasted_iota(jnp.int32, (mid, mid), 1) <= lax.broadcasted_iota(
        jnp.int32, (mid, mid), 0
    )

    def weigh(qs, ks):
        half = dot_t(qs, ks) * scale
        return 2.0 * half * (0.5 + 0.5 * jnp.tanh(half))

    low = jnp.where(keep, weigh(q[:mid], k[:mid]), 0.0).astype(BF16)
    cross = weigh(q[mid:], k[:mid]).astype(BF16)
    high = jnp.where(keep, weigh(q[mid:], k[mid:]), 0.0).astype(BF16)
    attn[head, :mid] = dot(low, v[:mid])
    attn[head, mid:] = dot(cross, v[:mid]) + dot(high, v[mid:])


def add_out(layer, outs, m, proj, attn, x, normed):
    w = out_matrix(outs, m)
    rows = 128
    for i in range(L // rows):
        r = pl.ds(i * rows, rows)
        a = jnp.concatenate([attn[h, r] for h in range(HEADS)], axis=1)
        u = jnp.concatenate([proj[h, r] for h in range(HEADS)], axis=1)
        gated = (layer_norm(a, EPS * L * L) * u.astype(F32)).astype(BF16)
        new = x[r] + dot(gated, w)
        if layer == 0:
            x[r] = new
            normed[r] = layer_norm(new).astype(BF16)
        else:
            x[r] = layer_norm(new)


def interest_vectors(outs, x):
    per = L // INTR
    rows = [jnp.sum(x[i * per : (i + 1) * per], axis=0, keepdims=True) / per for i in range(INTR)]
    pooled = layer_norm(jnp.concatenate(rows * (D // 128), axis=0))
    made = dot(pooled.astype(BF16), out_matrix(outs, 2))
    row = lax.broadcasted_iota(jnp.int32, (INTR * D // 128, 128), 0) // INTR
    packed = made[:, :128]
    for j in range(1, D // 128):
        packed = jnp.where(row == j, made[:, j * 128 : (j + 1) * 128], packed)
    return packed.astype(BF16)


def slot_rows(expand):
    r = lax.broadcasted_iota(jnp.int32, (128, 128), 0)
    c = lax.broadcasted_iota(jnp.int32, (128, 128), 1)
    same = jnp.logical_and(r // 16 == c // 16, (r // CAND) % INTR == c % INTR)
    for j in range(D // 128):
        expand[j * 128 : (j + 1) * 128] = jnp.where(
            jnp.logical_and(same, (c // INTR) % (D // 128) == j), 1.0, 0.0
        ).astype(BF16)


def decode(first, last, codes, codebook, cents, decoded):
    if first == 0:
        for s in range(SUB):
            cents[s] = codebook[s].astype(F32)

    @pl.loop(first, last)
    def _(blk):
        for s in range(SUB):
            code = jnp.broadcast_to(codes[blk, s : s + 1], (8, BS))
            spot = code & 127
            made = []
            for part in range(SD // 8):
                r = slice(part * 8, part * 8 + 8)
                low = jnp.take_along_axis(cents[s, r, :128], spot, axis=1)
                high = jnp.take_along_axis(cents[s, r, 128:], spot, axis=1)
                made.append(jnp.where(code < 128, low, high))
            decoded[blk, s * SD : (s + 1) * SD] = jnp.concatenate(made, axis=0).astype(BF16)


def live_slots(cand, counts, mine):
    mine[...] = jnp.zeros_like(mine)
    cnt = jnp.broadcast_to(counts[...].astype(F32), (CAND, INTR * ITEMS))
    slot = lax.broadcasted_iota(jnp.int32, (CAND, ITEMS), 0).astype(F32)
    rows = []
    for k in range(INTR):
        own = cnt[:, k * ITEMS : (k + 1) * ITEMS]
        rows.append(jnp.where(slot < own, cand[0, k].astype(F32), -1.0))
    mine[:, :ITEMS] = jnp.concatenate(rows, axis=0)


def kernel(
    hist_h, act_h, table_h, win_h, wout_h, wint_h, codebook_h, codes_h, cand_h, counts_h,
    out,
    hist, act, table, win, wout, wint, codebook, codes, cand, counts,
    weights, outs, own_rows, got_rows, shard,
    x, normed, proj, attn, cents, decoded,
    slots_mine, slots_got, wanted, expand, vec_mine, vec_got, res_mine,
    in_sem, mid_sem, late_sem,
    ex_s, ex_r, z_s, z_r, p_s, p1_r, p2_r, f_r, m_s, m_r, i_s, i_r, b_s, b_r,
):
    item, fsdp = lax.axis_index("item"), lax.axis_index("fsdp")
    y, x_lo = item // XL, item % XL
    z, x_hi, c = fsdp // (2 * XH), (fsdp // 2) % XH, fsdp % 2
    zq, zr = z // 4, z % 4
    xx = x_hi * XL + x_lo
    s = c * 2 + x_lo
    partner = (item, fsdp + 1 - 2 * c)

    def at_z(to):
        return (item, to * (2 * XH) + x_hi * 2 + c)

    def x_peer(off):
        to = lax.rem(xx + off, XS)
        return (y * XL + to % XL, z * (2 * XH) + (to // XL) * 2 + c)

    def y_peer(off):
        return (lax.rem(y + off, YS) * XL + x_lo, fsdp)

    def item_peer(off):
        return (lax.rem(item + off, ITEMS), fsdp)

    def copy(src, dst, send, recv, to):
        return pltpu.make_async_remote_copy(
            src_ref=src, dst_ref=dst, send_sem=send, recv_sem=recv, device_id=to, device_id_type=MESH
        )

    barrier = pltpu.get_barrier_semaphore()
    near = [partner] + [item_peer(o) for o in range(1, ITEMS)]
    near += [(y * XL + lo, z * (2 * XH) + (1 - x_hi) * 2 + c) for lo in range(XL)]
    own_quarter = [at_z(zq * ZP + lax.rem(z + o, ZP)) for o in range(1, ZP)]
    sibling = [at_z((zq + 1 - 2 * (zq % 2)) * ZP + t) for t in range(ZP)]
    planes = [at_z(t) for t in range(ZS)]

    def greet(sem, peers):
        for peer in peers:
            pl.semaphore_signal(sem, inc=1, device_id=peer, device_id_type=MESH)

    def if_quarter(which, act):
        pl.when({0: zq == 0, 1: zq == 1, 2: zq >= 2}[which])(act)

    EARLY, MID, LATE = range(3)

    operands = [
        (win_h, win), (wout_h, wout), (wint_h, wint), (hist_h, hist), (act_h, act), (table_h, table),
        (codebook_h, codebook), (codes_h, codes), (cand_h, cand), (counts_h, counts),
    ]
    fetches = [pltpu.make_async_copy(h, v, in_sem.at[i]) for i, (h, v) in enumerate(operands)]
    for t in fetches[:3]:
        t.start()
    greet(barrier, near + own_quarter)
    if_quarter(EARLY, lambda: greet(barrier, planes[ZP:]))
    if_quarter(MID, lambda: greet(barrier, planes[2 * ZP :]))
    if_quarter(LATE, lambda: greet(barrier, sibling))

    for t in fetches[3:]:
        t.start()

    def spread(dst0, value):
        value = value.astype(F32)
        for j in range(value.shape[1] // 128):
            own_rows[dst0 + j] = value[:, j * 128 : (j + 1) * 128]

    fetches[0].wait()
    spread(0, win[0])

    def prepare(last):
        for t in fetches[3:]:
            t.wait()
        live_slots(cand, counts, slots_mine)
        slot_rows(expand)
        start_values(hist, act, table, x, normed)
        decode(0, last, codes, codebook, cents, decoded)

    first = jnp.logical_and(z <= 1, item + fsdp > 0)
    pl.when(first)(lambda: prepare(NB))
    count = len(near) + ZP - 1
    if_quarter(EARLY, lambda: pl.semaphore_wait(barrier, count))
    if_quarter(MID, lambda: pl.semaphore_wait(barrier, count + ZP))
    if_quarter(LATE, lambda: pl.semaphore_wait(barrier, count + 3 * ZP))

    spans = [(0, IN_BLKS), (IN_BLKS, ALL_BLKS)]
    trades = [
        copy(own_rows.at[a:b], got_rows.at[a:b], ex_s.at[i], ex_r.at[i], partner)
        for i, (a, b) in enumerate(spans)
    ]
    trades[0].start()

    if_quarter(MID, lambda: greet(mid_sem, planes[:ZP]))
    if_quarter(LATE, lambda: greet(late_sem, planes[: 2 * ZP]))

    spread(IN_BLKS, win[1])
    fetches[1].wait()
    spread(2 * IN_BLKS, wout[0])
    spread(2 * IN_BLKS + OUT_BLKS, wout[1])
    fetches[2].wait()
    spread(2 * IN_BLKS + 2 * OUT_BLKS, wint[...])
    trades[1].start()

    def assemble(a, b):
        for j in range(a, b):
            mine, theirs = own_rows[j], got_rows[j]
            first = jnp.where(c == 0, mine, theirs)
            second = jnp.where(c == 0, theirs, mine)
            shard[j] = jnp.concatenate([first, second], axis=0).astype(BF16)

    blk = jnp.where(c == 0, y * 2 + x_lo, 8 + x_lo * 4 + y)
    shard_outs = shard.at[2 * IN_BLKS :].reshape(3, OUT_BLKS, 16, 128)

    def z_ends(chunk):
        if chunk < 2:
            return shard.at[chunk * IN_BLKS + blk], weights.at[chunk, blk, z, x_hi]
        m = slice(*OUT_PART[chunk])
        return shard_outs.at[m, y], outs.at[m, y, zq, zr, x_hi]

    def z_send(chunk, to):
        copy(*z_ends(chunk), z_s.at[chunk], z_r.at[chunk, zq], at_z(to)).start()

    def z_keep(chunk):
        src, dst = z_ends(chunk)
        pltpu.make_async_copy(src, dst, z_r.at[chunk, zq]).start()

    def if_has(chunk, act):
        if chunk < 2:
            act()
        else:
            pl.when(zr == s)(act)

    def z_to(chunk, first, last):
        def act():
            for t in range(first, last):
                z_send(chunk, t)

        if_has(chunk, act)

    def z_near(chunk):
        if_quarter(MID, lambda: z_to(chunk, 0, ZP))
        if_quarter(LATE, lambda: z_to(chunk, 0, 2 * ZP))

        def act():
            z_keep(chunk)
            for t in range(ZP - 1):
                z_send(chunk, zq * ZP + t + jnp.where(t >= zr, 1, 0))

            @pl.when(zq >= 2)
            def _():
                for t in range(ZP):
                    z_send(chunk, (zq + 1 - 2 * (zq % 2)) * ZP + t)

        if_has(chunk, act)

    def group(chunk, n_in, n_out):
        if chunk < 2:
            return weights.reshape(2 * IN_BLKS * ZS * XH, 16, 128).at[:n_in]
        first, last = OUT_PART[chunk]
        return outs.reshape(3 * OUT_BLKS * ZS * XH, 16, 128).at[: n_out * (last - first)]

    trades[0].wait_recv()
    assemble(*spans[0])
    z_near(0)
    pl.when(zq >= 2)(lambda: prepare(NB // 2))
    trades[1].wait_recv()
    assemble(*spans[1])
    for chunk in ORDER[1:]:
        z_near(chunk)

    pl.when(jnp.logical_and(zq <= 1, jnp.logical_not(first)))(lambda: prepare(NB))
    pl.when(zq >= 2)(lambda: decode(NB // 2, NB, codes, codebook, cents, decoded))

    slots_got[item] = slots_mine[...]
    slot_copies = [
        copy(slots_mine, slots_got.at[item], m_s, m_r, item_peer(o))
        for o in range(1, ITEMS)
    ]
    for t in slot_copies:
        t.start()

    def first_peer(off):
        xp, yp = x_peer(off), y_peer(off)
        return (jnp.where(c == 0, xp[0], yp[0]), jnp.where(c == 0, xp[1], yp[1]))

    def part(chunk, q):
        if chunk < 2:
            return weights.at[chunk, blk, pl.ds(q * ZP, ZP), x_hi]
        return outs.at[slice(*OUT_PART[chunk]), y, q, s, x_hi]

    def piece(which, chunk, q, off):
        if which == 0:
            at_y = lax.rem(y + YS - off, YS)
            if chunk < 2:
                return weights.at[chunk, pl.ds(at_y * 2, 2), pl.ds(q * ZP, ZP)]
            return outs.at[slice(*OUT_PART[chunk]), at_y, q, 0:2]
        at_x = lax.rem(xx + XS - off, XS)
        lo, hi = at_x % XL, at_x // XL
        if chunk < 2:
            return weights.at[chunk, pl.ds(8 + lo * 4, 4), pl.ds(q * ZP, ZP), hi]
        return outs.at[slice(*OUT_PART[chunk]), :, q, 2 + lo, hi]

    def piece_part(which, chunk, q, off, n):
        ref = piece(which, chunk, q, off)
        if chunk < 2:
            many = 1 if which == 0 else 2
            return ref.at[n * many : (n + 1) * many]
        return ref.at[:, n] if which == 0 else ref.at[:, 2 * n : 2 * n + 2]

    def core_half(which, chunk, q):
        if chunk < 2:
            return weights.at[chunk, which * 8 : which * 8 + 8, pl.ds(q * ZP, ZP)]
        return outs.at[slice(*OUT_PART[chunk]), :, q, which * 2 : which * 2 + 2]

    def by_core(act):
        pl.when(c == 0)(lambda: act(0))
        pl.when(c == 1)(lambda: act(1))

    def after_z(chunk, q):
        ref = part(chunk, q)
        copy(ref, ref, p_s.at[chunk], z_r.at[chunk, q], partner).wait_recv()
        for off in (2, 1, 3):
            copy(ref, ref, p_s.at[chunk], p1_r.at[chunk, q], first_peer(off)).start()

    def after_step1(chunk, q, ring=False):
        ref = group(chunk, 3 * ZP, 3)
        copy(ref, ref, p_s.at[chunk], p1_r.at[chunk, q], partner).wait_recv()

        def act(which):
            ref = piece(which, chunk, q, 0)
            peer = y_peer if which == 0 else x_peer
            for off in (1, 3) if ring else (2, 1, 3):
                copy(ref, ref, p_s.at[chunk], p2_r.at[chunk, q, off - 1], peer(off)).start()
            copy(ref, ref, p_s.at[chunk], f_r.at[chunk, q], partner).start()

        by_core(act)

    def pass_on(which, chunk, q, off):
        ref = piece(which, chunk, q, off)
        copy(ref, ref, p_s.at[chunk], p2_r.at[chunk, q, off - 1], partner).wait_recv()
        copy(ref, ref, p_s.at[chunk], f_r.at[chunk, q], partner).start()

    def after_step2(chunk, q):
        def act(which):
            for off in (1, 3, 2):
                pass_on(which, chunk, q, off)

        by_core(act)

    def after_near(chunk, q):
        def act(which):
            peer = y_peer if which == 0 else x_peer
            for off in (1, 3):
                pass_on(which, chunk, q, off)
                on = piece_part(which, chunk, q, off, off // 2)
                copy(on, on, p_s.at[chunk], p2_r.at[chunk, q, 1], peer(off)).start()

        by_core(act)

    def after_far(chunk, q):
        by_core(lambda which: pass_on(which, chunk, q, 2))

    def after_forward(chunk):
        for q in range(ZS // ZP):

            def act(which, q=q):
                ref = core_half(1 - which, chunk, q)
                copy(ref, ref, p_s.at[chunk], f_r.at[chunk, q], partner).wait_recv()

            by_core(act)

    q0, q1 = zq, zq + 1 - 2 * (zq % 2)
    q2 = 2 * (1 - zq // 2)

    def each(act, *pairs):
        for q, chunk in pairs:
            act(chunk, q)

    def z_of(*pairs):
        each(after_z, *pairs)

    def step1_of(*pairs):
        each(after_step1, *pairs)

    def ring1_of(*pairs):
        each(functools.partial(after_step1, ring=True), *pairs)

    def step2_of(*pairs):
        each(after_step2, *pairs)

    def near_of(*pairs):
        each(after_near, *pairs)

    def far_of(*pairs):
        each(after_far, *pairs)

    own = [(q0, chunk) for chunk in ORDER]
    sib = [(q1, chunk) for chunk in ORDER]

    def both(chunk):
        return (q0, chunk), (q1, chunk)

    def half(chunk):
        return (q2, chunk), (q2 + 1, chunk)

    def late_rows():
        pl.semaphore_wait(late_sem, 2 * ZP)
        z_to(IN0, 2 * ZP, ZS)

    @pl.when(zq <= 1)
    def _():
        z_of(*own)

        @pl.when(zq == 0)
        def _():
            pl.semaphore_wait(mid_sem, ZP)
            for chunk in ORDER:
                z_to(chunk, ZP, 2 * ZP)

        pl.when(zq == 1)(late_rows)
        ring1_of(*own)
        z_of(*sib)
        pl.when(zq == 0)(late_rows)
        near_of(*own)
        for chunk in ORDER[1:]:
            z_to(chunk, 2 * ZP, ZS)
        z_of(*half(IN0))
        ring1_of(*sib)
        far_of(*own)
        step1_of(*half(IN0))
        z_of(*half(OUT0))
        near_of(*sib)
        z_of(*half(IN1))
        step1_of(*half(OUT0))
        far_of((q1, IN0), (q1, OUT0))
        step2_of(*half(IN0))
        step1_of(*half(IN1))
        far_of((q1, IN1), (q1, OUT1))

    @pl.when(zq >= 2)
    def _():
        z_of(*both(IN0))
        z_of(*both(OUT0))
        step1_of(*both(IN0))
        z_of(*both(IN1))
        ring1_of(*both(OUT0))
        z_of(*half(IN0))
        step2_of(*both(IN0))
        ring1_of(*both(IN1))
        near_of(*both(OUT0))
        z_of(*both(OUT1))
        step1_of(*half(IN0))
        z_of(*half(OUT0))
        far_of(*both(OUT0))
        near_of(*both(IN1))
        z_of(*half(IN1))
        step1_of(*half(OUT0))
        ring1_of(*both(OUT1))
        step2_of(*half(IN0))
        far_of(*both(IN1))
        step1_of(*half(IN1))
        near_of(*both(OUT1))

    def all_got(got, sem):
        ref = got.at[: ITEMS - 1]
        copy(ref, ref, p_s.at[0], sem, partner).wait_recv()

    all_got(slots_got, m_r)
    rows = ITEMS * INTR * CAND
    lane = lax.broadcasted_iota(jnp.int32, (rows, 128), 1)
    picked = jnp.where(lane == item, slots_got[...].reshape(rows, 128), 0.0)
    wanted[...] = jnp.broadcast_to(jnp.sum(picked, axis=1, keepdims=True), (rows, 128))

    after_forward(IN0)
    for pair in range(8):
        project(0, pair, weights, normed, proj)
    z_of(*half(OUT1))
    step2_of(*half(OUT0))
    for head in range(HEADS):
        attend(head, proj, attn)
    step1_of(*half(OUT1))
    after_forward(OUT0)
    add_out(0, outs, 0, proj, attn, x, normed)
    step2_of(*half(IN1))
    after_forward(IN1)
    for pair in range(8):
        project(1, pair, weights, normed, proj)
    pl.when(zq >= 2)(lambda: far_of(*both(OUT1)))
    step2_of(*half(OUT1))
    for head in range(HEADS):
        attend(head, proj, attn)
    after_forward(OUT1)
    add_out(1, outs, 1, proj, attn, x, normed)

    vec = interest_vectors(outs, x)
    vec_mine[...] = vec
    vec_copies = [
        copy(vec_mine, vec_got.at[item], i_s, i_r, item_peer(o)) for o in range(1, ITEMS)
    ]
    for t in vec_copies:
        t.start()
    vec_got[item] = vec

    def all_left(sent, sem):
        ref = sent.at[: ITEMS - 1]
        copy(ref, ref, sem, i_r, partner).wait_send()

    for t in trades:
        t.wait_send()
    all_left(slots_got, m_s)
    for chunk in range(4):

        def left(chunk=chunk):
            ref = group(chunk, ZS - 1, ZS - 1)
            copy(ref, ref, z_s.at[chunk], i_r, partner).wait_send()

        if_has(chunk, left)
        ref = group(chunk, 4 * 124, 4 * 31)
        copy(ref, ref, p_s.at[chunk], i_r, partner).wait_send()

    all_got(vec_got, i_r)
    spread_out = dot(expand[...], vec_got[...].reshape(128, 128)).astype(BF16)
    all_vec = jnp.concatenate([spread_out[j * rows : (j + 1) * rows] for j in range(D // 128)], axis=1)
    chosen = jnp.zeros((rows, BS), F32)
    for pair in range(NB // 2):
        items = jnp.concatenate([decoded[2 * pair], decoded[2 * pair + 1]], axis=1)
        scored = dot(all_vec, items)
        want = wanted[...]
        chosen = jnp.where(want == float(2 * pair), scored[:, :BS], chosen)
        chosen = jnp.where(want == float(2 * pair + 1), scored[:, BS:], chosen)
    res_mine[...] = chosen.reshape(ITEMS, INTR * CAND, BS)

    for o in range(1, ITEMS):
        to = lax.rem(item + o, ITEMS)
        copy(res_mine.at[to], out.at[item], b_s, b_r, item_peer(o)).start()
    pltpu.make_async_copy(res_mine.at[item], out.at[item], b_r).start()
    all_left(vec_got, i_s)
    copy(out, out, b_s, b_r, partner).wait_recv()
    all_left(res_mine, b_s)


def body(history, actions, action_table, w_in, w_out, w_int, codebook, codes, cand, counts):
    hbm = pl.BlockSpec(memory_space=pltpu.HBM)
    dma = pltpu.SemaphoreType.DMA
    operands = (
        history, actions, action_table, w_in, w_out, w_int,
        jnp.transpose(codebook, (0, 2, 1)),
        jnp.transpose(codes, (0, 2, 1)),
        jnp.transpose(cand, (0, 1, 3, 2)),
        counts,
    )
    made = pl.pallas_call(
        kernel,
        out_shape=jax.ShapeDtypeStruct((ITEMS, INTR * CAND, BS), F32),
        in_specs=[hbm] * 10,
        out_specs=hbm,
        scratch_shapes=[pltpu.VMEM(a.shape, a.dtype) for a in operands]
        + [
            pltpu.VMEM((2, IN_BLKS, ZS, XH, 16, 128), BF16),
            pltpu.VMEM((3, OUT_BLKS, 4, 4, XH, 16, 128), BF16),
            pltpu.VMEM((ALL_BLKS, 8, 128), F32),
            pltpu.VMEM((ALL_BLKS, 8, 128), F32),
            pltpu.VMEM((ALL_BLKS, 16, 128), BF16),
            pltpu.VMEM((L, D), F32),
            pltpu.VMEM((L, D), BF16),
            pltpu.VMEM((IN_BLKS, L, 128), BF16),
            pltpu.VMEM((HEADS, L, HD), F32),
            pltpu.VMEM((SUB, SD, CENT), F32),
            pltpu.VMEM((NB, D, BS), BF16),
            pltpu.VMEM((INTR * CAND, 128), F32),
            pltpu.VMEM((ITEMS, INTR * CAND, 128), F32),
            pltpu.VMEM((ITEMS * INTR * CAND, 128), F32),
            pltpu.VMEM((D, 128), BF16),
            pltpu.VMEM((16, 128), BF16),
            pltpu.VMEM((ITEMS, 16, 128), BF16),
            pltpu.VMEM((ITEMS, INTR * CAND, BS), F32),
            dma((len(operands),)),
            pltpu.SemaphoreType.REGULAR,
            pltpu.SemaphoreType.REGULAR,
            dma((2,)),
            dma((2,)),
            dma((4,)),
            dma((4, 4)),
            dma((4,)),
            dma((4, 4)),
            dma((4, 4, 3)),
            dma((4, 4)),
        ]
        + [dma(())] * 6,
        compiler_params=pltpu.CompilerParams(
            collective_id=0, has_side_effects=True, vmem_limit_bytes=56 * 1024 * 1024
        ),
        name="encode_and_score",
    )(*operands)
    made = made.reshape(ITEMS, INTR, CAND, BS)
    return jnp.transpose(made, (1, 0, 2, 3))[None]


def solution(mesh):
    placed = (
        P(("item", "fsdp"), None, None),
        P(("item", "fsdp"), None),
        P(),
        P(None, "fsdp", None),
        P(None, "fsdp", None),
        P("fsdp", None),
        P(),
        P("item", None, None),
        P(("item", "fsdp"), None, None, None),
        P(("item", "fsdp"), None),
    )
    return jax.shard_map(
        body,
        mesh=mesh,
        in_specs=placed,
        out_specs=P(("item", "fsdp"), None, None, None, None),
        check_vma=False,
    )
```

```python
import functools
import math

import jax
import jax.numpy as jnp
from jax import lax
from jax.experimental import pallas as pl
from jax.experimental.pallas import tpu as pltpu
from jax.sharding import PartitionSpec as P

MESH = pl.DeviceIdType.MESH
F32 = jnp.float32
BF16 = jnp.bfloat16

YS, XL, XH, ZS = 4, 2, 2, 16
XS = XL * XH
ITEMS = YS * XL

D = 512
L = 512
HEADS = 4
HD = 128
ACTIONS = 16
SUB, SD, CENT = 32, 16, 256
NB, BS, CAND, INTR = 16, 128, 4, 4
EPS = 1e-05

IN_BLKS = 16
OUT_BLKS = 4
ALL_BLKS = 2 * IN_BLKS + 3 * OUT_BLKS
ZP = 4
IN0, IN1, OUT0, OUT1 = range(4)
ORDER = (IN0, OUT0, IN1, OUT1)
OUT_PART = {OUT0: (0, 1), OUT1: (1, 3)}


def layer_norm(value, eps=EPS):
    mean = jnp.mean(value, axis=-1, keepdims=True)
    centred = value - mean
    var = jnp.mean(centred * centred, axis=-1, keepdims=True)
    return centred * lax.rsqrt(var + eps)


def dot(a, b):
    return lax.dot_general(a, b, (((1,), (0,)), ((), ())), preferred_element_type=F32)


def dot_t(a, b):
    return lax.dot_general(a, b, (((1,), (1,)), ((), ())), preferred_element_type=F32)


def start_values(hist, act, table, x, normed):
    onehot = (
        lax.broadcasted_iota(jnp.int32, (ACTIONS, L), 0) == jnp.broadcast_to(act[...], (ACTIONS, L))
    ).astype(F32)
    rows = 128
    for i in range(L // rows):
        oh = onehot[:, i * rows : (i + 1) * rows].T.astype(BF16)
        part = hist[0, i * rows : (i + 1) * rows].astype(F32) + dot(oh, table[...])
        x[i * rows : (i + 1) * rows] = part
        normed[i * rows : (i + 1) * rows] = layer_norm(part).astype(BF16)


def in_block(weights, layer, blk):
    return weights[layer, blk].reshape(D, 128)


def out_matrix(outs, m):
    return jnp.concatenate([outs[m, j].reshape(D, 128) for j in range(OUT_BLKS)], axis=1)


def project(layer, pair, weights, normed, proj):
    w = jnp.concatenate(
        [in_block(weights, layer, 2 * pair), in_block(weights, layer, 2 * pair + 1)], axis=1
    )
    made = dot(normed[...], w)
    half = 0.5 * made
    made = (half * (1.0 + jnp.tanh(half))).astype(BF16)
    proj[2 * pair] = made[:, :128]
    proj[2 * pair + 1] = made[:, 128:]


def attend(head, proj, attn):
    v, q, k = proj[4 + head], proj[8 + head], proj[12 + head]
    scale = 0.5 / math.sqrt(HD)
    mid = L // 2
    keep = lax.broadcasted_iota(jnp.int32, (mid, mid), 1) <= lax.broadcasted_iota(
        jnp.int32, (mid, mid), 0
    )

    def weigh(qs, ks):
        half = dot_t(qs, ks) * scale
        return 2.0 * half * (0.5 + 0.5 * jnp.tanh(half))

    low = jnp.where(keep, weigh(q[:mid], k[:mid]), 0.0).astype(BF16)
    cross = weigh(q[mid:], k[:mid]).astype(BF16)
    high = jnp.where(keep, weigh(q[mid:], k[mid:]), 0.0).astype(BF16)
    attn[head, :mid] = dot(low, v[:mid])
    attn[head, mid:] = dot(cross, v[:mid]) + dot(high, v[mid:])


def add_out(layer, outs, m, proj, attn, x, normed):
    w = out_matrix(outs, m)
    rows = 128
    for i in range(L // rows):
        r = pl.ds(i * rows, rows)
        a = jnp.concatenate([attn[h, r] for h in range(HEADS)], axis=1)
        u = jnp.concatenate([proj[h, r] for h in range(HEADS)], axis=1)
        gated = (layer_norm(a, EPS * L * L) * u.astype(F32)).astype(BF16)
        new = x[r] + dot(gated, w)
        if layer == 0:
            x[r] = new
            normed[r] = layer_norm(new).astype(BF16)
        else:
            x[r] = layer_norm(new)


def make_tables(outs, x, codebook, tables):
    per = L // INTR
    rows = [jnp.sum(x[i * per : (i + 1) * per], axis=0, keepdims=True) / per for i in range(INTR)]
    pooled = layer_norm(jnp.concatenate(rows + rows, axis=0)).astype(BF16)
    interests = dot(pooled, out_matrix(outs, 2)).astype(BF16).astype(F32)
    sub = lax.broadcasted_iota(jnp.int32, (SUB, D), 0)
    feature = lax.broadcasted_iota(jnp.int32, (SUB, D), 1)
    apart = jnp.concatenate(
        [
            jnp.where(feature // SD == sub, jnp.broadcast_to(interests[k : k + 1], (SUB, D)), 0.0)
            for k in range(INTR)
        ],
        axis=0,
    ).astype(BF16)
    made = dot(apart, codebook[...].reshape(SUB * SD, CENT))
    tables[...] = made.astype(BF16).astype(F32)


def score(tables, codes_all, cand, counts, out):
    for k in range(INTR):
        low = [tables[k * SUB + 8 * i : k * SUB + 8 * i + 8, :128] for i in range(SUB // 8)]
        high = [tables[k * SUB + 8 * i : k * SUB + 8 * i + 8, 128:] for i in range(SUB // 8)]
        for g in range(ITEMS):
            live = counts[0, k * ITEMS + g]
            for b in range(CAND):
                blk = g * NB + jnp.clip(cand[0, k, b, g], 0, NB - 1)
                total = None
                for i in range(SUB // 8):
                    code = codes_all[blk, 8 * i : 8 * i + 8]
                    spot = code & 127
                    value = jnp.where(
                        code < 128,
                        jnp.take_along_axis(low[i], spot, axis=1),
                        jnp.take_along_axis(high[i], spot, axis=1),
                    )
                    total = value if total is None else total + value
                scored = jnp.sum(total, axis=0, keepdims=True)
                out[k, g, b : b + 1] = jnp.where(b < live, scored, 0.0)


def kernel(
    hist_h, act_h, table_h, win_h, wout_h, wint_h, codebook_h, codes_h, cand_h, counts_h,
    out,
    hist, act, table, win, wout, wint, codebook, codes, cand, counts,
    weights, outs, own_rows, got_rows, shard,
    x, normed, proj, attn, codes_got, codes_all, tables,
    in_sem, mid_sem, late_sem,
    ex_s, ex_r, z_s, z_r, p_s, p1_r, p2_r, f_r, c_s, c_r,
):
    item, fsdp = lax.axis_index("item"), lax.axis_index("fsdp")
    y, x_lo = item // XL, item % XL
    z, x_hi, c = fsdp // (2 * XH), (fsdp // 2) % XH, fsdp % 2
    zq, zr = z // 4, z % 4
    xx = x_hi * XL + x_lo
    s = c * 2 + x_lo
    partner = (item, fsdp + 1 - 2 * c)

    def at_z(to):
        return (item, to * (2 * XH) + x_hi * 2 + c)

    def x_peer(off):
        to = lax.rem(xx + off, XS)
        return (y * XL + to % XL, z * (2 * XH) + (to // XL) * 2 + c)

    def y_peer(off):
        return (lax.rem(y + off, YS) * XL + x_lo, fsdp)

    def copy(src, dst, send, recv, to):
        return pltpu.make_async_remote_copy(
            src_ref=src, dst_ref=dst, send_sem=send, recv_sem=recv, device_id=to, device_id_type=MESH
        )

    barrier = pltpu.get_barrier_semaphore()
    near = [partner] + [x_peer(o) for o in range(1, XS)] + [y_peer(o) for o in range(1, YS)]
    own_quarter = [at_z(zq * ZP + lax.rem(z + o, ZP)) for o in range(1, ZP)]
    sibling = [at_z((zq + 1 - 2 * (zq % 2)) * ZP + t) for t in range(ZP)]
    planes = [at_z(t) for t in range(ZS)]

    def greet(sem, peers):
        for peer in peers:
            pl.semaphore_signal(sem, inc=1, device_id=peer, device_id_type=MESH)

    def if_quarter(which, act):
        pl.when({0: zq == 0, 1: zq == 1, 2: zq >= 2}[which])(act)

    EARLY, MID, LATE = range(3)

    operands = [
        (win_h, win), (wout_h, wout), (wint_h, wint), (hist_h, hist), (act_h, act), (table_h, table),
        (codebook_h, codebook), (codes_h, codes), (cand_h, cand), (counts_h, counts),
    ]
    fetches = [pltpu.make_async_copy(h, v, in_sem.at[i]) for i, (h, v) in enumerate(operands)]
    for t in fetches[:3]:
        t.start()
    greet(barrier, near + own_quarter)
    if_quarter(EARLY, lambda: greet(barrier, planes[ZP:]))
    if_quarter(MID, lambda: greet(barrier, planes[2 * ZP :]))
    if_quarter(LATE, lambda: greet(barrier, sibling))

    for t in fetches[3:]:
        t.start()

    def spread(dst0, value):
        value = value.astype(F32)
        for j in range(value.shape[1] // 128):
            own_rows[dst0 + j] = value[:, j * 128 : (j + 1) * 128]

    fetches[0].wait()
    spread(0, win[0])

    def prepare():
        for t in fetches[3:]:
            t.wait()
        codes_got[y, x_lo, pl.ds(c * 8, 8)] = codes[pl.ds(c * 8, 8)].astype(F32).astype(BF16)
        start_values(hist, act, table, x, normed)

    first = jnp.logical_and(z <= 1, item + fsdp > 0)
    pl.when(first)(prepare)
    count = len(near) + ZP - 1
    if_quarter(EARLY, lambda: pl.semaphore_wait(barrier, count))
    if_quarter(MID, lambda: pl.semaphore_wait(barrier, count + ZP))
    if_quarter(LATE, lambda: pl.semaphore_wait(barrier, count + 3 * ZP))

    spans = [(0, IN_BLKS), (IN_BLKS, ALL_BLKS)]
    trades = [
        copy(own_rows.at[a:b], got_rows.at[a:b], ex_s.at[i], ex_r.at[i], partner)
        for i, (a, b) in enumerate(spans)
    ]
    trades[0].start()

    if_quarter(MID, lambda: greet(mid_sem, planes[:ZP]))
    if_quarter(LATE, lambda: greet(late_sem, planes[: 2 * ZP]))

    spread(IN_BLKS, win[1])
    fetches[1].wait()
    spread(2 * IN_BLKS, wout[0])
    spread(2 * IN_BLKS + OUT_BLKS, wout[1])
    fetches[2].wait()
    spread(2 * IN_BLKS + 2 * OUT_BLKS, wint[...])
    trades[1].start()

    def assemble(a, b):
        for j in range(a, b):
            mine, theirs = own_rows[j], got_rows[j]
            first = jnp.where(c == 0, mine, theirs)
            second = jnp.where(c == 0, theirs, mine)
            shard[j] = jnp.concatenate([first, second], axis=0).astype(BF16)

    blk = jnp.where(c == 0, y * 2 + x_lo, 8 + x_lo * 4 + y)
    shard_outs = shard.at[2 * IN_BLKS :].reshape(3, OUT_BLKS, 16, 128)

    def z_ends(chunk):
        if chunk < 2:
            return shard.at[chunk * IN_BLKS + blk], weights.at[chunk, blk, z, x_hi]
        m = slice(*OUT_PART[chunk])
        return shard_outs.at[m, y], outs.at[m, y, zq, zr, x_hi]

    def z_send(chunk, to):
        copy(*z_ends(chunk), z_s.at[chunk], z_r.at[chunk, zq], at_z(to)).start()

    def z_keep(chunk):
        src, dst = z_ends(chunk)
        pltpu.make_async_copy(src, dst, z_r.at[chunk, zq]).start()

    def if_has(chunk, act):
        if chunk < 2:
            act()
        else:
            pl.when(zr == s)(act)

    def z_to(chunk, first, last):
        def act():
            for t in range(first, last):
                z_send(chunk, t)

        if_has(chunk, act)

    def z_near(chunk):
        if_quarter(MID, lambda: z_to(chunk, 0, ZP))

        def act():
            z_keep(chunk)
            for t in range(ZP - 1):
                z_send(chunk, zq * ZP + t + jnp.where(t >= zr, 1, 0))

            @pl.when(zq >= 2)
            def _():
                for t in range(ZP):
                    z_send(chunk, (zq + 1 - 2 * (zq % 2)) * ZP + t)

        if_has(chunk, act)
        if_quarter(LATE, lambda: z_to(chunk, 0, 2 * ZP))

    def group(chunk, n_in, n_out):
        if chunk < 2:
            return weights.reshape(2 * IN_BLKS * ZS * XH, 16, 128).at[:n_in]
        first, last = OUT_PART[chunk]
        return outs.reshape(3 * OUT_BLKS * ZS * XH, 16, 128).at[: n_out * (last - first)]

    trades[0].wait_recv()
    assemble(*spans[0])
    z_near(0)
    pl.when(zq >= 2)(prepare)
    trades[1].wait_recv()
    assemble(*spans[1])
    for chunk in ORDER[1:]:
        z_near(chunk)

    pl.when(jnp.logical_and(zq <= 1, jnp.logical_not(first)))(prepare)

    other_lo = (item + 1 - 2 * x_lo, fsdp)

    def codes_copy(ref, to, stage):
        return copy(ref, ref, c_s, c_r.at[stage], to)

    def codes_first():
        @pl.when(c == 0)
        def _():
            codes_copy(codes_got.at[y, x_lo, 0:8], other_lo, 0).start()

        @pl.when(c == 1)
        def _():
            for off in (2, 1, 3):
                codes_copy(codes_got.at[y, x_lo, 8:16], y_peer(off), 0).start()

    def codes_second():
        @pl.when(c == 0)
        def _():
            codes_copy(codes_got.at[y, 1 - x_lo, 0:8], partner, 0).wait_recv()
            for off in (2, 1, 3):
                codes_copy(codes_got.at[y, :, 0:8], y_peer(off), 1).start()

        @pl.when(c == 1)
        def _():
            codes_copy(codes_got.at[0:3, 0, 8:16], partner, 0).wait_recv()
            codes_copy(codes_got.at[:, x_lo, 8:16], other_lo, 1).start()

    def codes_third():
        @pl.when(c == 0)
        def _():
            codes_copy(codes_got.at[0:3, :, 0:8], partner, 1).wait_recv()
            codes_copy(codes_got.at[:, :, 0:8], partner, 2).start()

        @pl.when(c == 1)
        def _():
            codes_copy(codes_got.at[:, 0, 8:16], partner, 1).wait_recv()
            codes_copy(codes_got.at[:, :, 8:16], partner, 2).start()

    def codes_last():
        pl.when(c == 0)(lambda: codes_copy(codes_got.at[:, :, 8:16], partner, 2).wait_recv())
        pl.when(c == 1)(lambda: codes_copy(codes_got.at[:, :, 0:8], partner, 2).wait_recv())
        for at_y in range(YS):
            for lo in range(XL):

                @pl.loop(0, NB)
                def _(i, at_y=at_y, lo=lo):
                    codes_all[(at_y * XL + lo) * NB + i] = codes_got[at_y, lo, i].astype(F32).astype(jnp.int32)

    codes_first()

    def first_peer(off):
        xp, yp = x_peer(off), y_peer(off)
        return (jnp.where(c == 0, xp[0], yp[0]), jnp.where(c == 0, xp[1], yp[1]))

    def part(chunk, q):
        if chunk < 2:
            return weights.at[chunk, blk, pl.ds(q * ZP, ZP), x_hi]
        return outs.at[slice(*OUT_PART[chunk]), y, q, s, x_hi]

    def piece(which, chunk, q, off):
        if which == 0:
            at_y = lax.rem(y + YS - off, YS)
            if chunk < 2:
                return weights.at[chunk, pl.ds(at_y * 2, 2), pl.ds(q * ZP, ZP)]
            return outs.at[slice(*OUT_PART[chunk]), at_y, q, 0:2]
        at_x = lax.rem(xx + XS - off, XS)
        lo, hi = at_x % XL, at_x // XL
        if chunk < 2:
            return weights.at[chunk, pl.ds(8 + lo * 4, 4), pl.ds(q * ZP, ZP), hi]
        return outs.at[slice(*OUT_PART[chunk]), :, q, 2 + lo, hi]

    def piece_part(which, chunk, q, off, n):
        ref = piece(which, chunk, q, off)
        if chunk < 2:
            many = 1 if which == 0 else 2
            return ref.at[n * many : (n + 1) * many]
        return ref.at[:, n] if which == 0 else ref.at[:, 2 * n : 2 * n + 2]

    def core_half(which, chunk, q):
        if chunk < 2:
            return weights.at[chunk, which * 8 : which * 8 + 8, pl.ds(q * ZP, ZP)]
        return outs.at[slice(*OUT_PART[chunk]), :, q, which * 2 : which * 2 + 2]

    def by_core(act):
        pl.when(c == 0)(lambda: act(0))
        pl.when(c == 1)(lambda: act(1))

    def after_z(chunk, q):
        ref = part(chunk, q)
        copy(ref, ref, p_s.at[chunk], z_r.at[chunk, q], partner).wait_recv()
        for off in (2, 1, 3):
            copy(ref, ref, p_s.at[chunk], p1_r.at[chunk, q], first_peer(off)).start()

    def after_step1(chunk, q, ring=False):
        ref = group(chunk, 3 * ZP, 3)
        copy(ref, ref, p_s.at[chunk], p1_r.at[chunk, q], partner).wait_recv()

        def act(which):
            ref = piece(which, chunk, q, 0)
            peer = y_peer if which == 0 else x_peer
            for off in (1, 3) if ring else (2, 1, 3):
                copy(ref, ref, p_s.at[chunk], p2_r.at[chunk, q, off - 1], peer(off)).start()
            copy(ref, ref, p_s.at[chunk], f_r.at[chunk, q], partner).start()

        by_core(act)

    def pass_on(which, chunk, q, off):
        ref = piece(which, chunk, q, off)
        copy(ref, ref, p_s.at[chunk], p2_r.at[chunk, q, off - 1], partner).wait_recv()
        copy(ref, ref, p_s.at[chunk], f_r.at[chunk, q], partner).start()

    def after_step2(chunk, q):
        def act(which):
            for off in (1, 3, 2):
                pass_on(which, chunk, q, off)

        by_core(act)

    def after_near(chunk, q):
        def act(which):
            peer = y_peer if which == 0 else x_peer
            for off in (1, 3):
                pass_on(which, chunk, q, off)
                on = piece_part(which, chunk, q, off, off // 2)
                copy(on, on, p_s.at[chunk], p2_r.at[chunk, q, 1], peer(off)).start()

        by_core(act)

    def after_far(chunk, q):
        by_core(lambda which: pass_on(which, chunk, q, 2))

    def after_forward(chunk):
        for q in range(ZS // ZP):

            def act(which, q=q):
                ref = core_half(1 - which, chunk, q)
                copy(ref, ref, p_s.at[chunk], f_r.at[chunk, q], partner).wait_recv()

            by_core(act)

    q0, q1 = zq, zq + 1 - 2 * (zq % 2)
    q2 = 2 * (1 - zq // 2)

    def each(act, *pairs):
        for q, chunk in pairs:
            act(chunk, q)

    def z_of(*pairs):
        each(after_z, *pairs)

    def step1_of(*pairs):
        each(after_step1, *pairs)

    def ring1_of(*pairs):
        each(functools.partial(after_step1, ring=True), *pairs)

    def step2_of(*pairs):
        each(after_step2, *pairs)

    def near_of(*pairs):
        each(after_near, *pairs)

    def far_of(*pairs):
        each(after_far, *pairs)

    own = [(q0, chunk) for chunk in ORDER]
    sib = [(q1, chunk) for chunk in ORDER]

    def both(chunk):
        return (q0, chunk), (q1, chunk)

    def half(chunk):
        return (q2, chunk), (q2 + 1, chunk)

    def late_rows():
        pl.semaphore_wait(late_sem, 2 * ZP)
        z_to(IN0, 2 * ZP, ZS)

    @pl.when(zq <= 1)
    def _():
        z_of(*own)
        codes_second()

        @pl.when(zq == 0)
        def _():
            pl.semaphore_wait(mid_sem, ZP)
            for chunk in ORDER:
                z_to(chunk, ZP, 2 * ZP)

        pl.when(zq == 1)(late_rows)
        ring1_of(*own)
        z_of(*sib)
        pl.when(zq == 0)(late_rows)
        codes_third()
        near_of(*own)
        z_of(*half(IN0))
        ring1_of(*sib)
        for chunk in ORDER[1:]:
            z_to(chunk, 2 * ZP, ZS)
        far_of(*own)
        codes_last()
        step1_of(*half(IN0))
        z_of(*half(OUT0))
        near_of(*sib)
        z_of(*half(IN1))
        step1_of(*half(OUT0))
        step1_of(*half(IN1))
        far_of((q1, IN0), (q1, OUT0))
        step2_of(*half(IN0))
        z_of(*half(OUT1))
        far_of((q1, IN1), (q1, OUT1))

    def if_late(act):
        pl.when(zq >= 2)(act)

    @if_late
    def _():
        z_of(*both(IN0))
        z_of(*both(OUT0))
        step1_of(*both(IN0))
        z_of(*both(IN1))
        ring1_of(*both(OUT0))
        step2_of(*both(IN0))
        ring1_of(*both(IN1))
        z_of(*half(IN0))
        near_of(*both(OUT0))
        z_of(*both(OUT1))
        near_of(*both(IN1))
        step1_of(*half(IN0))
        far_of(*both(OUT0))
        z_of(*half(OUT0))
        z_of(*half(IN1))
        ring1_of(*both(OUT1))
        far_of(*both(IN1))
        step1_of(*half(OUT0))
        step1_of(*half(IN1))
        step2_of(*half(IN0))
        near_of(*both(OUT1))
        codes_second()
        z_of(*half(OUT1))

    after_forward(IN0)
    for pair in range(8):
        project(0, pair, weights, normed, proj)
    step2_of(*half(OUT0))
    if_late(lambda: far_of(*both(OUT1)))
    for head in range(HEADS):
        attend(head, proj, attn)
    step1_of(*half(OUT1))
    step2_of(*half(IN1))
    after_forward(OUT0)
    add_out(0, outs, 0, proj, attn, x, normed)
    if_late(codes_third)
    after_forward(IN1)
    for pair in range(8):
        project(1, pair, weights, normed, proj)
    step2_of(*half(OUT1))
    for head in range(HEADS):
        attend(head, proj, attn)
    if_late(codes_last)
    after_forward(OUT1)
    add_out(1, outs, 1, proj, attn, x, normed)

    make_tables(outs, x, codebook, tables)
    score(tables, codes_all, cand, counts, out)

    for t in trades:
        t.wait_send()
    ref = codes_got.reshape(ITEMS * NB, SUB, BS).at[: 15 * 8]
    copy(ref, ref, c_s, c_r.at[0], partner).wait_send()
    for chunk in range(4):

        def left(chunk=chunk):
            ref = group(chunk, ZS - 1, ZS - 1)
            copy(ref, ref, z_s.at[chunk], c_r.at[0], partner).wait_send()

        if_has(chunk, left)
        ref = group(chunk, 4 * 124, 4 * 31)
        copy(ref, ref, p_s.at[chunk], c_r.at[0], partner).wait_send()


def body(history, actions, action_table, w_in, w_out, w_int, codebook, codes, cand, counts):
    hbm = pl.BlockSpec(memory_space=pltpu.HBM)
    dma = pltpu.SemaphoreType.DMA
    operands = (
        history, actions, action_table, w_in, w_out, w_int,
        jnp.transpose(codebook, (0, 2, 1)),
        jnp.transpose(codes, (0, 2, 1)),
        jnp.transpose(cand, (0, 1, 3, 2)),
        counts,
    )
    made = pl.pallas_call(
        kernel,
        out_shape=pltpu.VMEM((INTR, ITEMS, CAND, BS), F32),
        in_specs=[hbm] * 10,
        out_specs=pl.BlockSpec(memory_space=pltpu.VMEM),
        scratch_shapes=[pltpu.VMEM(a.shape, a.dtype) for a in operands[:8]]
        + [pltpu.SMEM(a.shape, a.dtype) for a in operands[8:]]
        + [
            pltpu.VMEM((2, IN_BLKS, ZS, XH, 16, 128), BF16),
            pltpu.VMEM((3, OUT_BLKS, 4, 4, XH, 16, 128), BF16),
            pltpu.VMEM((ALL_BLKS, 8, 128), F32),
            pltpu.VMEM((ALL_BLKS, 8, 128), F32),
            pltpu.VMEM((ALL_BLKS, 16, 128), BF16),
            pltpu.VMEM((L, D), F32),
            pltpu.VMEM((L, D), BF16),
            pltpu.VMEM((IN_BLKS, L, 128), BF16),
            pltpu.VMEM((HEADS, L, HD), F32),
            pltpu.VMEM((YS, XL, NB, SUB, BS), BF16),
            pltpu.VMEM((ITEMS * NB, SUB, BS), jnp.int32),
            pltpu.VMEM((INTR * SUB, CENT), F32),
            dma((len(operands),)),
            pltpu.SemaphoreType.REGULAR,
            pltpu.SemaphoreType.REGULAR,
            dma((2,)),
            dma((2,)),
            dma((4,)),
            dma((4, 4)),
            dma((4,)),
            dma((4, 4)),
            dma((4, 4, 3)),
            dma((4, 4)),
            dma(()),
            dma((3,)),
        ],
        compiler_params=pltpu.CompilerParams(
            collective_id=0, has_side_effects=True, vmem_limit_bytes=56 * 1024 * 1024
        ),
        name="encode_and_score",
    )(*operands)
    return made[None]


def solution(mesh):
    placed = (
        P(("item", "fsdp"), None, None),
        P(("item", "fsdp"), None),
        P(),
        P(None, "fsdp", None),
        P(None, "fsdp", None),
        P("fsdp", None),
        P(),
        P("item", None, None),
        P(("item", "fsdp"), None, None, None),
        P(("item", "fsdp"), None),
    )
    return jax.shard_map(
        body,
        mesh=mesh,
        in_specs=placed,
        out_specs=P(("item", "fsdp"), None, None, None, None),
        check_vma=False,
    )
```

```python
import functools
import math

import jax
import jax.numpy as jnp
from jax import lax
from jax.experimental import pallas as pl
from jax.experimental.pallas import tpu as pltpu
from jax.sharding import PartitionSpec as P

MESH = pl.DeviceIdType.MESH
F32 = jnp.float32
BF16 = jnp.bfloat16

YS, XL, XH, ZS = 4, 2, 2, 16
XS = XL * XH
ITEMS = YS * XL

D = 512
L = 512
HEADS = 4
HD = 128
ACTIONS = 16
SUB, SD, CENT = 32, 16, 256
NB, BS, CAND, INTR = 16, 128, 4, 4
EPS = 1e-05

IN_BLKS = 16
OUT_BLKS = 4
ALL_BLKS = 2 * IN_BLKS + 3 * OUT_BLKS
ZP = 4
IN0, IN1, OUT0, OUT1 = range(4)
ORDER = (IN0, OUT0, IN1, OUT1)
OUT_PART = {OUT0: (0, 1), OUT1: (1, 3)}


def layer_norm(value, eps=EPS):
    mean = jnp.mean(value, axis=-1, keepdims=True)
    centred = value - mean
    var = jnp.mean(centred * centred, axis=-1, keepdims=True)
    return centred * lax.rsqrt(var + eps)


def dot(a, b):
    return lax.dot_general(a, b, (((1,), (0,)), ((), ())), preferred_element_type=F32)


def dot_t(a, b):
    return lax.dot_general(a, b, (((1,), (1,)), ((), ())), preferred_element_type=F32)


def start_values(hist, act, table, x, normed):
    onehot = (
        lax.broadcasted_iota(jnp.int32, (ACTIONS, L), 0) == jnp.broadcast_to(act[...], (ACTIONS, L))
    ).astype(F32)
    rows = 128
    for i in range(L // rows):
        oh = onehot[:, i * rows : (i + 1) * rows].T.astype(BF16)
        part = hist[0, i * rows : (i + 1) * rows].astype(F32) + dot(oh, table[...])
        x[i * rows : (i + 1) * rows] = part
        normed[i * rows : (i + 1) * rows] = layer_norm(part).astype(BF16)


def in_block(weights, layer, blk):
    return weights[layer, blk].reshape(D, 128)


def out_matrix(outs, m):
    return jnp.concatenate([outs[m, j].reshape(D, 128) for j in range(OUT_BLKS)], axis=1)


def project(layer, pair, weights, normed, proj):
    w = jnp.concatenate(
        [in_block(weights, layer, 2 * pair), in_block(weights, layer, 2 * pair + 1)], axis=1
    )
    made = dot(normed[...], w)
    half = 0.5 * made
    made = (half * (1.0 + jnp.tanh(half))).astype(BF16)
    proj[2 * pair] = made[:, :128]
    proj[2 * pair + 1] = made[:, 128:]


def attend(head, proj, attn):
    v, q, k = proj[4 + head], proj[8 + head], proj[12 + head]
    scale = 0.5 / math.sqrt(HD)
    mid = L // 2
    keep = lax.broadcasted_iota(jnp.int32, (mid, mid), 1) <= lax.broadcasted_iota(
        jnp.int32, (mid, mid), 0
    )

    def weigh(qs, ks):
        half = dot_t(qs, ks) * scale
        return half * (1.0 + jnp.tanh(half))

    low = jnp.where(keep, weigh(q[:mid], k[:mid]), 0.0).astype(BF16)
    cross = weigh(q[mid:], k[:mid]).astype(BF16)
    high = jnp.where(keep, weigh(q[mid:], k[mid:]), 0.0).astype(BF16)
    attn[head, :mid] = dot(low, v[:mid])
    attn[head, mid:] = dot(cross, v[:mid]) + dot(high, v[mid:])


def add_out(layer, outs, m, proj, attn, x, normed):
    w = out_matrix(outs, m)
    rows = 128
    for i in range(L // rows):
        r = pl.ds(i * rows, rows)
        a = jnp.concatenate([attn[h, r] for h in range(HEADS)], axis=1)
        u = jnp.concatenate([proj[h, r] for h in range(HEADS)], axis=1)
        gated = (layer_norm(a, EPS * L * L) * u.astype(F32)).astype(BF16)
        new = x[r] + dot(gated, w)
        if layer == 0:
            x[r] = new
            normed[r] = layer_norm(new).astype(BF16)
        else:
            x[r] = layer_norm(new)


def make_tables(outs, x, codebook, tables):
    per = L // INTR
    rows = [jnp.sum(x[i * per : (i + 1) * per], axis=0, keepdims=True) / per for i in range(INTR)]
    pooled = layer_norm(jnp.concatenate(rows + rows, axis=0)).astype(BF16)
    interests = dot(pooled, out_matrix(outs, 2)).astype(BF16).astype(F32)
    sub = lax.broadcasted_iota(jnp.int32, (SUB, D), 0)
    feature = lax.broadcasted_iota(jnp.int32, (SUB, D), 1)
    apart = jnp.concatenate(
        [
            jnp.where(feature // SD == sub, jnp.broadcast_to(interests[k : k + 1], (SUB, D)), 0.0)
            for k in range(INTR)
        ],
        axis=0,
    ).astype(BF16)
    made = dot(apart, codebook[...].reshape(SUB * SD, CENT))
    tables[...] = made.astype(BF16).astype(F32)


def score(tables, codes, cand, counts, out):
    for k in range(INTR):
        low = [tables[k * SUB + 8 * i : k * SUB + 8 * i + 8, :128] for i in range(SUB // 8)]
        high = [tables[k * SUB + 8 * i : k * SUB + 8 * i + 8, 128:] for i in range(SUB // 8)]
        for g in range(ITEMS):
            live = counts[0, k * ITEMS + g]
            for b in range(CAND):
                blk = jnp.clip(cand[0, k, b, g], 0, NB - 1)
                item_codes = codes[g // XL, g % XL, blk].astype(F32).astype(jnp.int32)
                total = None
                for i in range(SUB // 8):
                    code = item_codes[8 * i : 8 * i + 8]
                    spot = code & 127
                    value = jnp.where(
                        code < 128,
                        jnp.take_along_axis(low[i], spot, axis=1),
                        jnp.take_along_axis(high[i], spot, axis=1),
                    )
                    total = value if total is None else total + value
                scored = jnp.sum(total, axis=0, keepdims=True)
                out[k, g, b : b + 1] = jnp.where(b < live, scored, 0.0)


def kernel(
    hist_h, act_h, table_h, win_h, wout_h, wint_h, codebook_h, codes_h, cand_h, counts_h,
    out,
    hist, act, table, win, wout, wint, codebook, codes, cand, counts,
    weights, outs, own_rows, got_rows, shard,
    x, normed, proj, attn, codes_got, tables,
    in_sem, mid_sem, late_sem,
    ex_s, ex_r, z_s, z_r, p_s, p1_r, p2_r, f_r, c_s, c_r,
):
    item, fsdp = lax.axis_index("item"), lax.axis_index("fsdp")
    y, x_lo = item // XL, item % XL
    z, x_hi, c = fsdp // (2 * XH), (fsdp // 2) % XH, fsdp % 2
    zq, zr = z // 4, z % 4
    xx = x_hi * XL + x_lo
    s = c * 2 + x_lo
    partner = (item, fsdp + 1 - 2 * c)

    def at_z(to):
        return (item, to * (2 * XH) + x_hi * 2 + c)

    def x_peer(off):
        to = lax.rem(xx + off, XS)
        return (y * XL + to % XL, z * (2 * XH) + (to // XL) * 2 + c)

    def y_peer(off):
        return (lax.rem(y + off, YS) * XL + x_lo, fsdp)

    def copy(src, dst, send, recv, to):
        return pltpu.make_async_remote_copy(
            src_ref=src, dst_ref=dst, send_sem=send, recv_sem=recv, device_id=to, device_id_type=MESH
        )

    barrier = pltpu.get_barrier_semaphore()
    near = [partner] + [x_peer(o) for o in range(1, XS)] + [y_peer(o) for o in range(1, YS)]
    own_quarter = [at_z(zq * ZP + lax.rem(z + o, ZP)) for o in range(1, ZP)]
    sibling = [at_z((zq + 1 - 2 * (zq % 2)) * ZP + t) for t in range(ZP)]
    planes = [at_z(t) for t in range(ZS)]

    def greet(sem, peers):
        for peer in peers:
            pl.semaphore_signal(sem, inc=1, device_id=peer, device_id_type=MESH)

    def if_quarter(which, act):
        pl.when({0: zq == 0, 1: zq == 1, 2: zq >= 2}[which])(act)

    EARLY, MID, LATE = range(3)

    operands = [
        (win_h, win), (wout_h, wout), (wint_h, wint), (hist_h, hist), (act_h, act), (table_h, table),
        (codebook_h, codebook), (codes_h, codes), (cand_h, cand), (counts_h, counts),
    ]
    fetches = [pltpu.make_async_copy(h, v, in_sem.at[i]) for i, (h, v) in enumerate(operands)]
    for t in fetches[:3]:
        t.start()
    greet(barrier, near + own_quarter)
    if_quarter(EARLY, lambda: greet(barrier, planes[ZP:]))
    if_quarter(MID, lambda: greet(barrier, planes[2 * ZP :]))
    if_quarter(LATE, lambda: greet(barrier, sibling))

    for t in fetches[3:]:
        t.start()

    def spread(dst0, value):
        value = value.astype(F32)
        for j in range(value.shape[1] // 128):
            own_rows[dst0 + j] = value[:, j * 128 : (j + 1) * 128]

    fetches[0].wait()
    spread(0, win[0])

    def prepare():
        for t in fetches[3:]:
            t.wait()
        codes_got[y, x_lo, pl.ds(c * 8, 8)] = codes[pl.ds(c * 8, 8)].astype(F32).astype(BF16)
        start_values(hist, act, table, x, normed)

    first = jnp.logical_and(z <= 1, item + fsdp > 0)
    pl.when(first)(prepare)
    count = len(near) + ZP - 1
    if_quarter(EARLY, lambda: pl.semaphore_wait(barrier, count))
    if_quarter(MID, lambda: pl.semaphore_wait(barrier, count + ZP))
    if_quarter(LATE, lambda: pl.semaphore_wait(barrier, count + 3 * ZP))

    spans = [(0, IN_BLKS), (IN_BLKS, ALL_BLKS)]
    trades = [
        copy(own_rows.at[a:b], got_rows.at[a:b], ex_s.at[i], ex_r.at[i], partner)
        for i, (a, b) in enumerate(spans)
    ]
    trades[0].start()

    if_quarter(MID, lambda: greet(mid_sem, planes[:ZP]))
    if_quarter(LATE, lambda: greet(late_sem, planes[: 2 * ZP]))

    spread(IN_BLKS, win[1])
    fetches[1].wait()
    spread(2 * IN_BLKS, wout[0])
    spread(2 * IN_BLKS + OUT_BLKS, wout[1])
    fetches[2].wait()
    spread(2 * IN_BLKS + 2 * OUT_BLKS, wint[...])
    trades[1].start()

    def assemble(a, b):
        for j in range(a, b):
            mine, theirs = own_rows[j], got_rows[j]
            first = jnp.where(c == 0, mine, theirs)
            second = jnp.where(c == 0, theirs, mine)
            shard[j] = jnp.concatenate([first, second], axis=0).astype(BF16)

    blk = jnp.where(c == 0, y * 2 + x_lo, 8 + x_lo * 4 + y)
    shard_outs = shard.at[2 * IN_BLKS :].reshape(3, OUT_BLKS, 16, 128)

    def z_ends(chunk):
        if chunk < 2:
            return shard.at[chunk * IN_BLKS + blk], weights.at[chunk, blk, z, x_hi]
        m = slice(*OUT_PART[chunk])
        return shard_outs.at[m, y], outs.at[m, y, zq, zr, x_hi]

    def z_send(chunk, to):
        copy(*z_ends(chunk), z_s.at[chunk], z_r.at[chunk, zq], at_z(to)).start()

    def z_keep(chunk):
        src, dst = z_ends(chunk)
        pltpu.make_async_copy(src, dst, z_r.at[chunk, zq]).start()

    def if_has(chunk, act):
        if chunk < 2:
            act()
        else:
            pl.when(zr == s)(act)

    def z_to(chunk, first, last):
        def act():
            for t in range(first, last):
                z_send(chunk, t)

        if_has(chunk, act)

    def z_near(chunk):
        if_quarter(MID, lambda: z_to(chunk, 0, ZP))

        def act():
            z_keep(chunk)
            for t in range(ZP - 1):
                z_send(chunk, zq * ZP + t + jnp.where(t >= zr, 1, 0))

            @pl.when(zq >= 2)
            def _():
                for t in range(ZP):
                    z_send(chunk, (zq + 1 - 2 * (zq % 2)) * ZP + t)

        if_has(chunk, act)
        if_quarter(LATE, lambda: z_to(chunk, 0, 2 * ZP))

    def group(chunk, n_in, n_out):
        if chunk < 2:
            return weights.reshape(2 * IN_BLKS * ZS * XH, 16, 128).at[:n_in]
        first, last = OUT_PART[chunk]
        return outs.reshape(3 * OUT_BLKS * ZS * XH, 16, 128).at[: n_out * (last - first)]

    trades[0].wait_recv()
    assemble(*spans[0])
    z_near(0)
    pl.when(zq >= 2)(prepare)
    trades[1].wait_recv()
    assemble(*spans[1])
    for chunk in ORDER[1:]:
        z_near(chunk)

    pl.when(jnp.logical_and(zq <= 1, jnp.logical_not(first)))(prepare)

    other_lo = (item + 1 - 2 * x_lo, fsdp)

    def codes_copy(ref, to, stage):
        return copy(ref, ref, c_s, c_r.at[stage], to)

    def codes_first():
        @pl.when(c == 0)
        def _():
            codes_copy(codes_got.at[y, x_lo, 0:8], other_lo, 0).start()

        @pl.when(c == 1)
        def _():
            for off in (2, 1, 3):
                codes_copy(codes_got.at[y, x_lo, 8:16], y_peer(off), 0).start()

    def codes_second():
        @pl.when(c == 0)
        def _():
            codes_copy(codes_got.at[y, 1 - x_lo, 0:8], partner, 0).wait_recv()
            for off in (2, 1, 3):
                codes_copy(codes_got.at[y, :, 0:8], y_peer(off), 1).start()

        @pl.when(c == 1)
        def _():
            codes_copy(codes_got.at[0:3, 0, 8:16], partner, 0).wait_recv()
            codes_copy(codes_got.at[:, x_lo, 8:16], other_lo, 1).start()

    def codes_third():
        @pl.when(c == 0)
        def _():
            codes_copy(codes_got.at[0:3, :, 0:8], partner, 1).wait_recv()
            codes_copy(codes_got.at[:, :, 0:8], partner, 2).start()

        @pl.when(c == 1)
        def _():
            codes_copy(codes_got.at[:, 0, 8:16], partner, 1).wait_recv()
            codes_copy(codes_got.at[:, :, 8:16], partner, 2).start()

    def codes_last():
        pl.when(c == 0)(lambda: codes_copy(codes_got.at[:, :, 8:16], partner, 2).wait_recv())
        pl.when(c == 1)(lambda: codes_copy(codes_got.at[:, :, 0:8], partner, 2).wait_recv())

    codes_first()

    def first_peer(off):
        xp, yp = x_peer(off), y_peer(off)
        return (jnp.where(c == 0, xp[0], yp[0]), jnp.where(c == 0, xp[1], yp[1]))

    def part(chunk, q):
        if chunk < 2:
            return weights.at[chunk, blk, pl.ds(q * ZP, ZP), x_hi]
        return outs.at[slice(*OUT_PART[chunk]), y, q, s, x_hi]

    def piece(which, chunk, q, off):
        if which == 0:
            at_y = lax.rem(y + YS - off, YS)
            if chunk < 2:
                return weights.at[chunk, pl.ds(at_y * 2, 2), pl.ds(q * ZP, ZP)]
            return outs.at[slice(*OUT_PART[chunk]), at_y, q, 0:2]
        at_x = lax.rem(xx + XS - off, XS)
        lo, hi = at_x % XL, at_x // XL
        if chunk < 2:
            return weights.at[chunk, pl.ds(8 + lo * 4, 4), pl.ds(q * ZP, ZP), hi]
        return outs.at[slice(*OUT_PART[chunk]), :, q, 2 + lo, hi]

    def piece_part(which, chunk, q, off, n):
        ref = piece(which, chunk, q, off)
        if chunk < 2:
            many = 1 if which == 0 else 2
            return ref.at[n * many : (n + 1) * many]
        return ref.at[:, n] if which == 0 else ref.at[:, 2 * n : 2 * n + 2]

    def core_half(which, chunk, q):
        if chunk < 2:
            return weights.at[chunk, which * 8 : which * 8 + 8, pl.ds(q * ZP, ZP)]
        return outs.at[slice(*OUT_PART[chunk]), :, q, which * 2 : which * 2 + 2]

    def by_core(act):
        pl.when(c == 0)(lambda: act(0))
        pl.when(c == 1)(lambda: act(1))

    def after_z(chunk, q):
        ref = part(chunk, q)
        copy(ref, ref, p_s.at[chunk], z_r.at[chunk, q], partner).wait_recv()
        for off in (2, 1, 3):
            copy(ref, ref, p_s.at[chunk], p1_r.at[chunk, q], first_peer(off)).start()

    def after_step1(chunk, q, ring=False):
        ref = group(chunk, 3 * ZP, 3)
        copy(ref, ref, p_s.at[chunk], p1_r.at[chunk, q], partner).wait_recv()

        def act(which):
            ref = piece(which, chunk, q, 0)
            peer = y_peer if which == 0 else x_peer
            for off in (1, 3) if ring else (2, 1, 3):
                copy(ref, ref, p_s.at[chunk], p2_r.at[chunk, q, off - 1], peer(off)).start()
            copy(ref, ref, p_s.at[chunk], f_r.at[chunk, q], partner).start()

        by_core(act)

    def pass_on(which, chunk, q, off):
        ref = piece(which, chunk, q, off)
        copy(ref, ref, p_s.at[chunk], p2_r.at[chunk, q, off - 1], partner).wait_recv()
        copy(ref, ref, p_s.at[chunk], f_r.at[chunk, q], partner).start()

    def after_step2(chunk, q):
        def act(which):
            for off in (1, 3, 2):
                pass_on(which, chunk, q, off)

        by_core(act)

    def after_near(chunk, q):
        def act(which):
            peer = y_peer if which == 0 else x_peer
            for off in (1, 3):
                pass_on(which, chunk, q, off)
                on = piece_part(which, chunk, q, off, off // 2)
                copy(on, on, p_s.at[chunk], p2_r.at[chunk, q, 1], peer(off)).start()

        by_core(act)

    def after_far(chunk, q):
        by_core(lambda which: pass_on(which, chunk, q, 2))

    def after_forward(chunk):
        for q in range(ZS // ZP):

            def act(which, q=q):
                ref = core_half(1 - which, chunk, q)
                copy(ref, ref, p_s.at[chunk], f_r.at[chunk, q], partner).wait_recv()

            by_core(act)

    q0, q1 = zq, zq + 1 - 2 * (zq % 2)
    q2 = 2 * (1 - zq // 2)

    def each(act, *pairs):
        for q, chunk in pairs:
            act(chunk, q)

    def z_of(*pairs):
        each(after_z, *pairs)

    def step1_of(*pairs):
        each(after_step1, *pairs)

    def ring1_of(*pairs):
        each(functools.partial(after_step1, ring=True), *pairs)

    def step2_of(*pairs):
        each(after_step2, *pairs)

    def near_of(*pairs):
        each(after_near, *pairs)

    def far_of(*pairs):
        each(after_far, *pairs)

    own = [(q0, chunk) for chunk in ORDER]
    sib = [(q1, chunk) for chunk in ORDER]

    def both(chunk):
        return (q0, chunk), (q1, chunk)

    def half(chunk):
        return (q2, chunk), (q2 + 1, chunk)

    def late_rows():
        pl.semaphore_wait(late_sem, 2 * ZP)
        z_to(IN0, 2 * ZP, ZS)

    codes_second()

    @pl.when(zq <= 1)
    def _():
        z_of(*own)

        @pl.when(zq == 0)
        def _():
            pl.semaphore_wait(mid_sem, ZP)
            for chunk in ORDER:
                z_to(chunk, ZP, 2 * ZP)

        pl.when(zq == 1)(late_rows)
        ring1_of(*own)
        z_of(*sib)
        pl.when(zq == 0)(late_rows)
        codes_third()
        near_of(*own)
        z_of(*half(IN0))
        ring1_of(*sib)
        for chunk in ORDER[1:]:
            z_to(chunk, 2 * ZP, ZS)
        far_of(*own)
        step1_of(*half(IN0))
        z_of(*half(OUT0))
        near_of(*sib)
        z_of(*half(IN1))
        step1_of(*half(OUT0))
        step1_of(*half(IN1))
        far_of((q1, IN0), (q1, OUT0))
        step2_of(*half(IN0))
        z_of(*half(OUT1))
        far_of((q1, IN1), (q1, OUT1))

    def if_late(act):
        pl.when(zq >= 2)(act)

    @if_late
    def _():
        z_of(*both(IN0))
        z_of(*both(OUT0))
        step1_of(*both(IN0))
        z_of(*both(IN1))
        ring1_of(*both(OUT0))
        codes_third()
        step2_of(*both(IN0))
        ring1_of(*both(IN1))
        z_of(*half(IN0))
        near_of(*both(OUT0))
        z_of(*both(OUT1))
        step1_of(*half(IN0))
        near_of(*both(IN1))
        far_of(*both(OUT0))
        z_of(*half(OUT0))
        z_of(*half(IN1))
        ring1_of(*both(OUT1))
        step1_of(*half(OUT0))
        step1_of(*half(IN1))
        z_of(*half(OUT1))
        far_of(*both(IN1))
        step2_of(*half(IN0))

    after_forward(IN0)
    for pair in range(8):
        project(0, pair, weights, normed, proj)

    if_late(lambda: near_of(*both(OUT1)))
    step2_of(*half(OUT0))
    for head in range(HEADS):
        attend(head, proj, attn)
    step1_of(*half(OUT1))
    step2_of(*half(IN1))
    after_forward(OUT0)
    add_out(0, outs, 0, proj, attn, x, normed)
    after_forward(IN1)
    for pair in range(8):
        project(1, pair, weights, normed, proj)
    if_late(lambda: far_of(*both(OUT1)))
    step2_of(*half(OUT1))
    for head in range(HEADS):
        attend(head, proj, attn)
    codes_last()
    after_forward(OUT1)
    add_out(1, outs, 1, proj, attn, x, normed)

    make_tables(outs, x, codebook, tables)
    score(tables, codes_got, cand, counts, out)

    for t in trades:
        t.wait_send()
    ref = codes_got.reshape(ITEMS * NB, SUB, BS).at[: 15 * 8]
    copy(ref, ref, c_s, c_r.at[0], partner).wait_send()
    for chunk in range(4):

        def left(chunk=chunk):
            ref = group(chunk, ZS - 1, ZS - 1)
            copy(ref, ref, z_s.at[chunk], c_r.at[0], partner).wait_send()

        if_has(chunk, left)
        ref = group(chunk, 4 * 124, 4 * 31)
        copy(ref, ref, p_s.at[chunk], c_r.at[0], partner).wait_send()


def body(history, actions, action_table, w_in, w_out, w_int, codebook, codes, cand, counts):
    hbm = pl.BlockSpec(memory_space=pltpu.HBM)
    dma = pltpu.SemaphoreType.DMA
    operands = (
        history, actions, action_table, w_in, w_out, w_int,
        jnp.transpose(codebook, (0, 2, 1)),
        jnp.transpose(codes, (0, 2, 1)),
        jnp.transpose(cand, (0, 1, 3, 2)),
        counts,
    )
    made = pl.pallas_call(
        kernel,
        out_shape=pltpu.VMEM((INTR, ITEMS, CAND, BS), F32),
        in_specs=[hbm] * 10,
        out_specs=pl.BlockSpec(memory_space=pltpu.VMEM),
        scratch_shapes=[pltpu.VMEM(a.shape, a.dtype) for a in operands[:8]]
        + [pltpu.SMEM(a.shape, a.dtype) for a in operands[8:]]
        + [
            pltpu.VMEM((2, IN_BLKS, ZS, XH, 16, 128), BF16),
            pltpu.VMEM((3, OUT_BLKS, 4, 4, XH, 16, 128), BF16),
            pltpu.VMEM((ALL_BLKS, 8, 128), F32),
            pltpu.VMEM((ALL_BLKS, 8, 128), F32),
            pltpu.VMEM((ALL_BLKS, 16, 128), BF16),
            pltpu.VMEM((L, D), F32),
            pltpu.VMEM((L, D), BF16),
            pltpu.VMEM((IN_BLKS, L, 128), BF16),
            pltpu.VMEM((HEADS, L, HD), F32),
            pltpu.VMEM((YS, XL, NB, SUB, BS), BF16),
            pltpu.VMEM((INTR * SUB, CENT), F32),
            dma((len(operands),)),
            pltpu.SemaphoreType.REGULAR,
            pltpu.SemaphoreType.REGULAR,
            dma((2,)),
            dma((2,)),
            dma((4,)),
            dma((4, 4)),
            dma((4,)),
            dma((4, 4)),
            dma((4, 4, 3)),
            dma((4, 4)),
            dma(()),
            dma((3,)),
        ],
        compiler_params=pltpu.CompilerParams(
            collective_id=0, has_side_effects=True, vmem_limit_bytes=56 * 1024 * 1024
        ),
        name="encode_and_score",
    )(*operands)
    return made[None]


def solution(mesh):
    placed = (
        P(("item", "fsdp"), None, None),
        P(("item", "fsdp"), None),
        P(),
        P(None, "fsdp", None),
        P(None, "fsdp", None),
        P("fsdp", None),
        P(),
        P("item", None, None),
        P(("item", "fsdp"), None, None, None),
        P(("item", "fsdp"), None),
    )
    return jax.shard_map(
        body,
        mesh=mesh,
        in_specs=placed,
        out_specs=P(("item", "fsdp"), None, None, None, None),
        check_vma=False,
    )
```

```python
import functools
import math

import jax
import jax.numpy as jnp
from jax import lax
from jax.experimental import pallas as pl
from jax.experimental.pallas import tpu as pltpu
from jax.sharding import PartitionSpec as P

MESH = pl.DeviceIdType.MESH
F32 = jnp.float32
BF16 = jnp.bfloat16

YS, XL, XH, ZS = 4, 2, 2, 16
XS = XL * XH
ITEMS = YS * XL

D = 512
L = 512
HEADS = 4
HD = 128
ACTIONS = 16
SUB, SD, CENT = 32, 16, 256
NB, BS, CAND, INTR = 16, 128, 4, 4
EPS = 1e-05

IN_BLKS = 16
OUT_BLKS = 4
ALL_BLKS = 2 * IN_BLKS + 3 * OUT_BLKS
ZP = 4
IN0, IN1, OUT0, OUT1 = range(4)
ORDER = (IN0, OUT0, IN1, OUT1)
OUT_PART = {OUT0: (0, 1), OUT1: (1, 3)}


def layer_norm(value, eps=EPS):
    mean = jnp.mean(value, axis=-1, keepdims=True)
    centred = value - mean
    var = jnp.mean(centred * centred, axis=-1, keepdims=True)
    return centred * lax.rsqrt(var + eps)


def dot(a, b):
    return lax.dot_general(a, b, (((1,), (0,)), ((), ())), preferred_element_type=F32)


def dot_t(a, b):
    return lax.dot_general(a, b, (((1,), (1,)), ((), ())), preferred_element_type=F32)


def start_values(hist, act, table, x, normed):
    onehot = (
        lax.broadcasted_iota(jnp.int32, (ACTIONS, L), 0) == jnp.broadcast_to(act[...], (ACTIONS, L))
    ).astype(F32)
    rows = 128
    for i in range(L // rows):
        oh = onehot[:, i * rows : (i + 1) * rows].T.astype(BF16)
        part = hist[0, i * rows : (i + 1) * rows].astype(F32) + dot(oh, table[...])
        x[i * rows : (i + 1) * rows] = part
        normed[i * rows : (i + 1) * rows] = layer_norm(part).astype(BF16)


def in_block(weights, layer, blk):
    return weights[layer, blk].reshape(D, 128)


def out_matrix(outs, m):
    return jnp.concatenate([outs[m, j].reshape(D, 128) for j in range(OUT_BLKS)], axis=1)


def project(layer, pair, weights, normed, proj):
    w = jnp.concatenate(
        [in_block(weights, layer, 2 * pair), in_block(weights, layer, 2 * pair + 1)], axis=1
    )
    made = dot(normed[...], w)
    half = 0.5 * made
    made = (half * (1.0 + jnp.tanh(half))).astype(BF16)
    proj[2 * pair] = made[:, :128]
    proj[2 * pair + 1] = made[:, 128:]


def attend(head, proj, attn):
    v, q, k = proj[4 + head], proj[8 + head], proj[12 + head]
    scale = 0.5 / math.sqrt(HD)
    mid = L // 2
    keep = lax.broadcasted_iota(jnp.int32, (mid, mid), 1) <= lax.broadcasted_iota(
        jnp.int32, (mid, mid), 0
    )

    def weigh(qs, ks):
        half = dot_t(qs, ks) * scale
        return half * (1.0 + jnp.tanh(half))

    low = jnp.where(keep, weigh(q[:mid], k[:mid]), 0.0).astype(BF16)
    cross = weigh(q[mid:], k[:mid]).astype(BF16)
    high = jnp.where(keep, weigh(q[mid:], k[mid:]), 0.0).astype(BF16)
    attn[head, :mid] = dot(low, v[:mid])
    attn[head, mid:] = dot(cross, v[:mid]) + dot(high, v[mid:])


def add_out(layer, outs, m, proj, attn, x, normed):
    w = out_matrix(outs, m)
    rows = L // INTR
    means = []
    for i in range(L // rows):
        r = pl.ds(i * rows, rows)
        a = jnp.concatenate([attn[h, r] for h in range(HEADS)], axis=1)
        u = jnp.concatenate([proj[h, r] for h in range(HEADS)], axis=1)
        gated = (layer_norm(a, EPS * L * L) * u.astype(F32)).astype(BF16)
        new = x[r] + dot(gated, w)
        if layer == 0:
            x[r] = new
            normed[r] = layer_norm(new).astype(BF16)
        else:
            means.append(jnp.sum(layer_norm(new), axis=0, keepdims=True) / rows)
    return means


def make_tables(outs, rows, codebook, tables):
    pooled = layer_norm(jnp.concatenate(rows + rows, axis=0)).astype(BF16)
    interests = dot(pooled, out_matrix(outs, 2)).astype(BF16).astype(F32)
    sub = lax.broadcasted_iota(jnp.int32, (SUB, D), 0)
    feature = lax.broadcasted_iota(jnp.int32, (SUB, D), 1)
    apart = jnp.concatenate(
        [
            jnp.where(feature // SD == sub, jnp.broadcast_to(interests[k : k + 1], (SUB, D)), 0.0)
            for k in range(INTR)
        ],
        axis=0,
    ).astype(BF16)
    made = dot(apart, codebook[...].reshape(SUB * SD, CENT))
    tables[...] = made.astype(BF16).astype(F32)


def score(tables, codes, cand, counts, out):
    for k in range(INTR):
        low = [tables[k * SUB + 8 * i : k * SUB + 8 * i + 8, :128] for i in range(SUB // 8)]
        high = [tables[k * SUB + 8 * i : k * SUB + 8 * i + 8, 128:] for i in range(SUB // 8)]
        for g in range(ITEMS):
            live = counts[0, k * ITEMS + g]
            for b in range(CAND):
                blk = jnp.clip(cand[0, k, b, g], 0, NB - 1)
                item_codes = codes[g // XL, g % XL, blk].astype(F32).astype(jnp.int32)
                total = None
                for i in range(SUB // 8):
                    code = item_codes[8 * i : 8 * i + 8]
                    spot = code & 127
                    value = jnp.where(
                        code < 128,
                        jnp.take_along_axis(low[i], spot, axis=1),
                        jnp.take_along_axis(high[i], spot, axis=1),
                    )
                    total = value if total is None else total + value
                scored = jnp.sum(total, axis=0, keepdims=True)
                out[k, g, b : b + 1] = jnp.where(b < live, scored, 0.0)


def kernel(
    hist_h, act_h, table_h, win_h, wout_h, wint_h, codebook_h, codes_h, cand_h, counts_h,
    out,
    hist, act, table, win, wout, wint, codebook, codes, cand, counts,
    weights, outs, own_rows, got_rows, shard,
    x, normed, proj, attn, codes_got, tables,
    in_sem, mid_sem, late_sem,
    ex_s, ex_r, z_s, z_r, p_s, p1_r, p2_r, f_r, c_s, c_r,
):
    item, fsdp = lax.axis_index("item"), lax.axis_index("fsdp")
    y, x_lo = item // XL, item % XL
    z, x_hi, c = fsdp // (2 * XH), (fsdp // 2) % XH, fsdp % 2
    zq, zr = z // 4, z % 4
    xx = x_hi * XL + x_lo
    s = c * 2 + x_lo
    partner = (item, fsdp + 1 - 2 * c)

    def at_z(to):
        return (item, to * (2 * XH) + x_hi * 2 + c)

    def x_peer(off):
        to = lax.rem(xx + off, XS)
        return (y * XL + to % XL, z * (2 * XH) + (to // XL) * 2 + c)

    def y_peer(off):
        return (lax.rem(y + off, YS) * XL + x_lo, fsdp)

    def copy(src, dst, send, recv, to):
        return pltpu.make_async_remote_copy(
            src_ref=src, dst_ref=dst, send_sem=send, recv_sem=recv, device_id=to, device_id_type=MESH
        )

    barrier = pltpu.get_barrier_semaphore()
    near = [partner] + [x_peer(o) for o in range(1, XS)] + [y_peer(o) for o in range(1, YS)]
    own_quarter = [at_z(zq * ZP + lax.rem(z + o, ZP)) for o in range(1, ZP)]
    sibling = [at_z((zq + 1 - 2 * (zq % 2)) * ZP + t) for t in range(ZP)]
    planes = [at_z(t) for t in range(ZS)]

    def greet(sem, peers):
        for peer in peers:
            pl.semaphore_signal(sem, inc=1, device_id=peer, device_id_type=MESH)

    def if_quarter(which, act):
        pl.when({0: zq == 0, 1: zq == 1, 2: zq >= 2}[which])(act)

    EARLY, MID, LATE = range(3)

    operands = [
        (win_h, win), (wout_h, wout), (wint_h, wint), (hist_h, hist), (act_h, act), (table_h, table),
        (codebook_h, codebook), (codes_h, codes), (cand_h, cand), (counts_h, counts),
    ]
    fetches = [pltpu.make_async_copy(h, v, in_sem.at[i]) for i, (h, v) in enumerate(operands)]
    for t in fetches[:3]:
        t.start()
    greet(barrier, near + own_quarter)
    if_quarter(EARLY, lambda: greet(barrier, planes[ZP:]))
    if_quarter(MID, lambda: greet(barrier, planes[2 * ZP :]))
    if_quarter(LATE, lambda: greet(barrier, sibling))

    for t in fetches[3:]:
        t.start()

    def spread(dst0, value):
        value = value.astype(F32)
        for j in range(value.shape[1] // 128):
            own_rows[dst0 + j] = value[:, j * 128 : (j + 1) * 128]

    fetches[0].wait()
    spread(0, win[0])

    def prepare():
        for t in fetches[3:]:
            t.wait()
        codes_got[y, x_lo, pl.ds(c * 8, 8)] = codes[pl.ds(c * 8, 8)].astype(F32).astype(BF16)
        start_values(hist, act, table, x, normed)

    first = jnp.logical_and(z <= 1, item + fsdp > 0)
    pl.when(first)(prepare)
    count = len(near) + ZP - 1
    if_quarter(EARLY, lambda: pl.semaphore_wait(barrier, count))
    if_quarter(MID, lambda: pl.semaphore_wait(barrier, count + ZP))
    if_quarter(LATE, lambda: pl.semaphore_wait(barrier, count + 3 * ZP))

    spans = [(0, IN_BLKS), (IN_BLKS, ALL_BLKS)]
    trades = [
        copy(own_rows.at[a:b], got_rows.at[a:b], ex_s.at[i], ex_r.at[i], partner)
        for i, (a, b) in enumerate(spans)
    ]
    trades[0].start()

    if_quarter(MID, lambda: greet(mid_sem, planes[:ZP]))
    if_quarter(LATE, lambda: greet(late_sem, planes[: 2 * ZP]))

    spread(IN_BLKS, win[1])
    fetches[1].wait()
    spread(2 * IN_BLKS, wout[0])
    spread(2 * IN_BLKS + OUT_BLKS, wout[1])
    fetches[2].wait()
    spread(2 * IN_BLKS + 2 * OUT_BLKS, wint[...])
    trades[1].start()

    def assemble(a, b):
        for j in range(a, b):
            mine, theirs = own_rows[j], got_rows[j]
            first = jnp.where(c == 0, mine, theirs)
            second = jnp.where(c == 0, theirs, mine)
            shard[j] = jnp.concatenate([first, second], axis=0).astype(BF16)

    blk = jnp.where(c == 0, y * 2 + x_lo, 8 + x_lo * 4 + y)
    shard_outs = shard.at[2 * IN_BLKS :].reshape(3, OUT_BLKS, 16, 128)

    def z_ends(chunk):
        if chunk < 2:
            return shard.at[chunk * IN_BLKS + blk], weights.at[chunk, blk, z, x_hi]
        m = slice(*OUT_PART[chunk])
        return shard_outs.at[m, y], outs.at[m, y, zq, zr, x_hi]

    def z_send(chunk, to):
        copy(*z_ends(chunk), z_s.at[chunk], z_r.at[chunk, zq], at_z(to)).start()

    def z_keep(chunk):
        src, dst = z_ends(chunk)
        pltpu.make_async_copy(src, dst, z_r.at[chunk, zq]).start()

    def if_has(chunk, act):
        if chunk < 2:
            act()
        else:
            pl.when(zr == s)(act)

    def z_to(chunk, first, last):
        def act():
            for t in range(first, last):
                z_send(chunk, t)

        if_has(chunk, act)

    def z_near(chunk):
        if_quarter(MID, lambda: z_to(chunk, 0, ZP))

        def act():
            z_keep(chunk)
            for t in range(ZP - 1):
                z_send(chunk, zq * ZP + t + jnp.where(t >= zr, 1, 0))

            @pl.when(zq >= 2)
            def _():
                for t in range(ZP):
                    z_send(chunk, (zq + 1 - 2 * (zq % 2)) * ZP + t)

        if_has(chunk, act)
        if_quarter(LATE, lambda: z_to(chunk, 0, 2 * ZP))

    def group(chunk, n_in, n_out):
        if chunk < 2:
            return weights.reshape(2 * IN_BLKS * ZS * XH, 16, 128).at[:n_in]
        first, last = OUT_PART[chunk]
        return outs.reshape(3 * OUT_BLKS * ZS * XH, 16, 128).at[: n_out * (last - first)]

    trades[0].wait_recv()
    assemble(*spans[0])
    z_near(0)
    pl.when(zq >= 2)(prepare)
    trades[1].wait_recv()
    assemble(*spans[1])
    for chunk in ORDER[1:]:
        z_near(chunk)

    pl.when(jnp.logical_and(zq <= 1, jnp.logical_not(first)))(prepare)

    other_lo = (item + 1 - 2 * x_lo, fsdp)

    def codes_copy(ref, to, stage):
        return copy(ref, ref, c_s, c_r.at[stage], to)

    def codes_first():
        @pl.when(c == 0)
        def _():
            codes_copy(codes_got.at[y, x_lo, 0:8], other_lo, 0).start()

        @pl.when(c == 1)
        def _():
            for off in (2, 1, 3):
                codes_copy(codes_got.at[y, x_lo, 8:16], y_peer(off), 0).start()

    def codes_second():
        @pl.when(c == 0)
        def _():
            codes_copy(codes_got.at[y, 1 - x_lo, 0:8], partner, 0).wait_recv()
            for off in (2, 1, 3):
                codes_copy(codes_got.at[y, :, 0:8], y_peer(off), 1).start()

        @pl.when(c == 1)
        def _():
            codes_copy(codes_got.at[0:3, 0, 8:16], partner, 0).wait_recv()
            codes_copy(codes_got.at[:, x_lo, 8:16], other_lo, 1).start()

    def codes_third():
        @pl.when(c == 0)
        def _():
            codes_copy(codes_got.at[0:3, :, 0:8], partner, 1).wait_recv()
            codes_copy(codes_got.at[:, :, 0:8], partner, 2).start()

        @pl.when(c == 1)
        def _():
            codes_copy(codes_got.at[:, 0, 8:16], partner, 1).wait_recv()
            codes_copy(codes_got.at[:, :, 8:16], partner, 2).start()

    def codes_last():
        pl.when(c == 0)(lambda: codes_copy(codes_got.at[:, :, 8:16], partner, 2).wait_recv())
        pl.when(c == 1)(lambda: codes_copy(codes_got.at[:, :, 0:8], partner, 2).wait_recv())

    codes_first()

    def first_peer(off):
        xp, yp = x_peer(off), y_peer(off)
        return (jnp.where(c == 0, xp[0], yp[0]), jnp.where(c == 0, xp[1], yp[1]))

    def part(chunk, q):
        if chunk < 2:
            return weights.at[chunk, blk, pl.ds(q * ZP, ZP), x_hi]
        return outs.at[slice(*OUT_PART[chunk]), y, q, s, x_hi]

    def piece(which, chunk, q, off):
        if which == 0:
            at_y = lax.rem(y + YS - off, YS)
            if chunk < 2:
                return weights.at[chunk, pl.ds(at_y * 2, 2), pl.ds(q * ZP, ZP)]
            return outs.at[slice(*OUT_PART[chunk]), at_y, q, 0:2]
        at_x = lax.rem(xx + XS - off, XS)
        lo, hi = at_x % XL, at_x // XL
        if chunk < 2:
            return weights.at[chunk, pl.ds(8 + lo * 4, 4), pl.ds(q * ZP, ZP), hi]
        return outs.at[slice(*OUT_PART[chunk]), :, q, 2 + lo, hi]

    def piece_part(which, chunk, q, off, n):
        ref = piece(which, chunk, q, off)
        if chunk < 2:
            many = 1 if which == 0 else 2
            return ref.at[n * many : (n + 1) * many]
        return ref.at[:, n] if which == 0 else ref.at[:, 2 * n : 2 * n + 2]

    def core_half(which, chunk):
        if chunk < 2:
            return weights.at[chunk, which * 8 : which * 8 + 8]
        return outs.at[slice(*OUT_PART[chunk]), :, :, which * 2 : which * 2 + 2]

    def by_core(act):
        pl.when(c == 0)(lambda: act(0))
        pl.when(c == 1)(lambda: act(1))

    def after_z(chunk, q):
        ref = part(chunk, q)
        copy(ref, ref, p_s.at[chunk], z_r.at[chunk, q], partner).wait_recv()
        for off in (2, 1, 3):
            copy(ref, ref, p_s.at[chunk], p1_r.at[chunk, q], first_peer(off)).start()

    def after_step1(chunk, q, ring=False):
        ref = group(chunk, 3 * ZP, 3)
        copy(ref, ref, p_s.at[chunk], p1_r.at[chunk, q], partner).wait_recv()

        def act(which):
            ref = piece(which, chunk, q, 0)
            peer = y_peer if which == 0 else x_peer
            for off in (1, 3) if ring else (2, 1, 3):
                copy(ref, ref, p_s.at[chunk], p2_r.at[chunk, q, 1 - off % 2], peer(off)).start()
            pass_on(which, chunk, q, 0)

        by_core(act)

    def pass_on(which, chunk, q, off):
        ref = piece(which, chunk, q, off)
        copy(ref, ref, p_s.at[chunk], f_r.at[chunk], partner).start()

    def got_near(chunk, q):
        ref = group(chunk, 8 * ZP, 8)
        copy(ref, ref, p_s.at[chunk], p2_r.at[chunk, q, 0], partner).wait_recv()

    def after_near(chunk, q):
        def act(which):
            peer = y_peer if which == 0 else x_peer
            for off in (1, 3):
                on = piece_part(which, chunk, q, off, off // 2)
                copy(on, on, p_s.at[chunk], p2_r.at[chunk, q, 1], peer(off)).start()
            for off in (1, 3):
                pass_on(which, chunk, q, off)

        got_near(chunk, q)
        by_core(act)

    def after_far(chunk, q):
        def act(which):
            ref = piece(which, chunk, q, 2)
            copy(ref, ref, p_s.at[chunk], p2_r.at[chunk, q, 1], partner).wait_recv()
            pass_on(which, chunk, q, 2)

        by_core(act)

    def after_step2(chunk, q):
        def act(which):
            pass_on(which, chunk, q, 1)
            pass_on(which, chunk, q, 3)

        got_near(chunk, q)
        by_core(act)
        after_far(chunk, q)

    def after_forward(chunk):
        def act(which):
            ref = core_half(1 - which, chunk)
            copy(ref, ref, p_s.at[chunk], f_r.at[chunk], partner).wait_recv()

        by_core(act)

    q0, q1 = zq, zq + 1 - 2 * (zq % 2)
    q2 = 2 * (1 - zq // 2)

    def each(act, *pairs):
        for q, chunk in pairs:
            act(chunk, q)

    def z_of(*pairs):
        each(after_z, *pairs)

    def step1_of(*pairs):
        each(after_step1, *pairs)

    def ring1_of(*pairs):
        each(functools.partial(after_step1, ring=True), *pairs)

    def step2_of(*pairs):
        each(after_step2, *pairs)

    def near_of(*pairs):
        each(after_near, *pairs)

    def far_of(*pairs):
        each(after_far, *pairs)

    own = [(q0, chunk) for chunk in ORDER]
    sib = [(q1, chunk) for chunk in ORDER]

    def both(chunk):
        return (q0, chunk), (q1, chunk)

    def half(chunk):
        return (q2, chunk), (q2 + 1, chunk)

    def late_rows():
        pl.semaphore_wait(late_sem, 2 * ZP)
        z_to(IN0, 2 * ZP, ZS)

    codes_second()

    @pl.when(zq <= 1)
    def _():
        z_of(*own)

        @pl.when(zq == 0)
        def _():
            pl.semaphore_wait(mid_sem, ZP)
            for chunk in ORDER:
                z_to(chunk, ZP, 2 * ZP)

        pl.when(zq == 1)(late_rows)
        ring1_of(*own)
        z_of(*sib)
        pl.when(zq == 0)(late_rows)
        codes_third()
        near_of(*own)
        z_of(*half(IN0))
        step1_of(*sib[:1])
        ring1_of(*sib[1:])
        for chunk in ORDER[1:]:
            z_to(chunk, 2 * ZP, ZS)
        far_of(*own)
        step1_of(*half(IN0))
        z_of(*half(OUT0))
        step2_of(*sib[:1])
        near_of(*sib[1:])
        z_of(*half(IN1))
        step1_of(*half(OUT0))
        step1_of(*half(IN1))
        far_of((q1, OUT0))
        step2_of(*half(IN0))
        z_of(*half(OUT1))
        far_of((q1, IN1), (q1, OUT1))

    def if_late(act):
        pl.when(zq >= 2)(act)

    @if_late
    def _():
        z_of(*both(IN0))
        z_of(*both(OUT0))
        step1_of(*both(IN0))
        z_of(*both(IN1))
        ring1_of(*both(OUT0))
        codes_third()
        step2_of(*both(IN0))
        ring1_of(*both(IN1))
        z_of(*half(IN0))
        near_of(*both(OUT0))
        z_of(*both(OUT1))
        step1_of(*half(IN0))
        near_of(*both(IN1))
        far_of(*both(OUT0))
        z_of(*half(OUT0))
        z_of(*half(IN1))
        ring1_of(*both(OUT1))
        step1_of(*half(OUT0))
        step1_of(*half(IN1))
        z_of(*half(OUT1))
        far_of(*both(IN1))
        step2_of(*half(IN0))

    for pair in range(4):
        project(0, 4 * c + pair, weights, normed, proj)
    after_forward(IN0)
    for pair in range(4):
        project(0, 4 - 4 * c + pair, weights, normed, proj)

    if_late(lambda: near_of(*both(OUT1)))
    step2_of(*half(OUT0))
    for head in range(HEADS):
        attend(head, proj, attn)
    step1_of(*half(OUT1))
    step2_of(*half(IN1))
    after_forward(OUT0)
    add_out(0, outs, 0, proj, attn, x, normed)
    for pair in range(4):
        project(1, 4 * c + pair, weights, normed, proj)
    after_forward(IN1)
    for pair in range(4):
        project(1, 4 - 4 * c + pair, weights, normed, proj)
    if_late(lambda: far_of(*both(OUT1)))
    step2_of(*half(OUT1))
    for head in range(HEADS):
        attend(head, proj, attn)
    codes_last()
    after_forward(OUT1)
    means = add_out(1, outs, 1, proj, attn, x, normed)

    make_tables(outs, means, codebook, tables)
    score(tables, codes_got, cand, counts, out)

    for t in trades:
        t.wait_send()
    ref = codes_got.reshape(ITEMS * NB, SUB, BS).at[: 15 * 8]
    copy(ref, ref, c_s, c_r.at[0], partner).wait_send()
    for chunk in range(4):

        def left(chunk=chunk):
            ref = group(chunk, ZS - 1, ZS - 1)
            copy(ref, ref, z_s.at[chunk], c_r.at[0], partner).wait_send()

        if_has(chunk, left)
        ref = group(chunk, 4 * 124, 4 * 31)
        copy(ref, ref, p_s.at[chunk], c_r.at[0], partner).wait_send()


def body(history, actions, action_table, w_in, w_out, w_int, codebook, codes, cand, counts):
    hbm = pl.BlockSpec(memory_space=pltpu.HBM)
    dma = pltpu.SemaphoreType.DMA
    operands = (
        history, actions, action_table, w_in, w_out, w_int,
        jnp.transpose(codebook, (0, 2, 1)),
        jnp.transpose(codes, (0, 2, 1)),
        jnp.transpose(cand, (0, 1, 3, 2)),
        counts,
    )
    made = pl.pallas_call(
        kernel,
        out_shape=pltpu.VMEM((INTR, ITEMS, CAND, BS), F32),
        in_specs=[hbm] * 10,
        out_specs=pl.BlockSpec(memory_space=pltpu.VMEM),
        scratch_shapes=[pltpu.VMEM(a.shape, a.dtype) for a in operands[:8]]
        + [pltpu.SMEM(a.shape, a.dtype) for a in operands[8:]]
        + [
            pltpu.VMEM((2, IN_BLKS, ZS, XH, 16, 128), BF16),
            pltpu.VMEM((3, OUT_BLKS, 4, 4, XH, 16, 128), BF16),
            pltpu.VMEM((ALL_BLKS, 8, 128), F32),
            pltpu.VMEM((ALL_BLKS, 8, 128), F32),
            pltpu.VMEM((ALL_BLKS, 16, 128), BF16),
            pltpu.VMEM((L, D), F32),
            pltpu.VMEM((L, D), BF16),
            pltpu.VMEM((IN_BLKS, L, 128), BF16),
            pltpu.VMEM((HEADS, L, HD), F32),
            pltpu.VMEM((YS, XL, NB, SUB, BS), BF16),
            pltpu.VMEM((INTR * SUB, CENT), F32),
            dma((len(operands),)),
            pltpu.SemaphoreType.REGULAR,
            pltpu.SemaphoreType.REGULAR,
            dma((2,)),
            dma((2,)),
            dma((4,)),
            dma((4, 4)),
            dma((4,)),
            dma((4, 4)),
            dma((4, 4, 2)),
            dma((4,)),
            dma(()),
            dma((3,)),
        ],
        compiler_params=pltpu.CompilerParams(
            collective_id=0, has_side_effects=True, vmem_limit_bytes=56 * 1024 * 1024
        ),
        name="encode_and_score",
    )(*operands)
    return made[None]


def solution(mesh):
    placed = (
        P(("item", "fsdp"), None, None),
        P(("item", "fsdp"), None),
        P(),
        P(None, "fsdp", None),
        P(None, "fsdp", None),
        P("fsdp", None),
        P(),
        P("item", None, None),
        P(("item", "fsdp"), None, None, None),
        P(("item", "fsdp"), None),
    )
    return jax.shard_map(
        body,
        mesh=mesh,
        in_specs=placed,
        out_specs=P(("item", "fsdp"), None, None, None, None),
        check_vma=False,
    )
```

```python
import functools
import math

import jax
import jax.numpy as jnp
from jax import lax
from jax.experimental import pallas as pl
from jax.experimental.pallas import tpu as pltpu
from jax.sharding import PartitionSpec as P

MESH = pl.DeviceIdType.MESH
F32 = jnp.float32
BF16 = jnp.bfloat16

YS, XL, XH, ZS = 4, 2, 2, 16
XS = XL * XH
ITEMS = YS * XL

D = 512
L = 512
HEADS = 4
HD = 128
ACTIONS = 16
SUB, SD, CENT = 32, 16, 256
NB, BS, CAND, INTR = 16, 128, 4, 4
EPS = 1e-05

IN_BLKS = 16
OUT_BLKS = 4
ALL_BLKS = 2 * IN_BLKS + 3 * OUT_BLKS
ZP = 4
IN0, IN1, OUT0, OUT1 = range(4)
ORDER = (IN0, OUT0, IN1, OUT1)
OUT_PART = {OUT0: (0, 1), OUT1: (1, 3)}


def layer_norm(value, eps=EPS):
    mean = jnp.mean(value, axis=-1, keepdims=True)
    centred = value - mean
    var = jnp.mean(centred * centred, axis=-1, keepdims=True)
    return centred * lax.rsqrt(var + eps)


def dot(a, b):
    return lax.dot_general(a, b, (((1,), (0,)), ((), ())), preferred_element_type=F32)


def dot_t(a, b):
    return lax.dot_general(a, b, (((1,), (1,)), ((), ())), preferred_element_type=F32)


def start_values(hist, act, table, x, normed):
    onehot = (
        lax.broadcasted_iota(jnp.int32, (ACTIONS, L), 0) == jnp.broadcast_to(act[...], (ACTIONS, L))
    ).astype(F32)
    rows = 128
    for i in range(L // rows):
        oh = onehot[:, i * rows : (i + 1) * rows].T.astype(BF16)
        part = hist[0, i * rows : (i + 1) * rows].astype(F32) + dot(oh, table[...])
        x[i * rows : (i + 1) * rows] = part
        normed[i * rows : (i + 1) * rows] = layer_norm(part).astype(BF16)


def in_block(weights, layer, blk):
    return weights[layer, blk].reshape(D, 128)


def out_matrix(outs, m):
    return jnp.concatenate([outs[m, j].reshape(D, 128) for j in range(OUT_BLKS)], axis=1)


def project(layer, pair, weights, normed, proj):
    w = jnp.concatenate(
        [in_block(weights, layer, 2 * pair), in_block(weights, layer, 2 * pair + 1)], axis=1
    )
    made = dot(normed[...], w)
    half = 0.5 * made
    made = (half * (1.0 + jnp.tanh(half))).astype(BF16)
    proj[2 * pair] = made[:, :128]
    proj[2 * pair + 1] = made[:, 128:]


def attend(head, proj, attn):
    v, q, k = proj[4 + head], proj[8 + head], proj[12 + head]
    scale = 0.5 / math.sqrt(HD)
    mid = L // 2
    keep = lax.broadcasted_iota(jnp.int32, (mid, mid), 1) <= lax.broadcasted_iota(
        jnp.int32, (mid, mid), 0
    )

    def weigh(qs, ks):
        half = dot_t(qs, ks) * scale
        return half * (1.0 + jnp.tanh(half))

    low = jnp.where(keep, weigh(q[:mid], k[:mid]), 0.0).astype(BF16)
    cross = weigh(q[mid:], k[:mid]).astype(BF16)
    high = jnp.where(keep, weigh(q[mid:], k[mid:]), 0.0).astype(BF16)
    attn[head, :mid] = dot(low, v[:mid])
    attn[head, mid:] = dot(cross, v[:mid]) + dot(high, v[mid:])


def add_out(layer, outs, m, proj, attn, x, normed):
    w = out_matrix(outs, m)
    rows = L // INTR
    means = []
    for i in range(L // rows):
        r = pl.ds(i * rows, rows)
        a = jnp.concatenate([attn[h, r] for h in range(HEADS)], axis=1)
        u = jnp.concatenate([proj[h, r] for h in range(HEADS)], axis=1)
        gated = (layer_norm(a, EPS * L * L) * u.astype(F32)).astype(BF16)
        new = x[r] + dot(gated, w)
        if layer == 0:
            x[r] = new
            normed[r] = layer_norm(new).astype(BF16)
        else:
            means.append(jnp.sum(layer_norm(new), axis=0, keepdims=True) / rows)
    return means


def make_tables(outs, rows, codebook, tables):
    pooled = layer_norm(jnp.concatenate(rows + rows, axis=0)).astype(BF16)
    interests = dot(pooled, out_matrix(outs, 2)).astype(BF16).astype(F32)
    sub = lax.broadcasted_iota(jnp.int32, (SUB, D), 0)
    feature = lax.broadcasted_iota(jnp.int32, (SUB, D), 1)
    apart = jnp.concatenate(
        [
            jnp.where(feature // SD == sub, jnp.broadcast_to(interests[k : k + 1], (SUB, D)), 0.0)
            for k in range(INTR)
        ],
        axis=0,
    ).astype(BF16)
    made = dot(apart, codebook[...].reshape(SUB * SD, CENT))
    tables[...] = made.astype(BF16).astype(F32)


def score(tables, codes, cand, counts, out):
    for k in range(INTR):
        low = [tables[k * SUB + 8 * i : k * SUB + 8 * i + 8, :128] for i in range(SUB // 8)]
        high = [tables[k * SUB + 8 * i : k * SUB + 8 * i + 8, 128:] for i in range(SUB // 8)]
        for g in range(ITEMS):
            live = counts[0, k * ITEMS + g]
            for b in range(CAND):
                blk = jnp.clip(cand[0, k, b, g], 0, NB - 1)
                item_codes = codes[g // XL, g % XL, blk].astype(F32).astype(jnp.int32)
                total = None
                for i in range(SUB // 8):
                    code = item_codes[8 * i : 8 * i + 8]
                    spot = code & 127
                    value = jnp.where(
                        code < 128,
                        jnp.take_along_axis(low[i], spot, axis=1),
                        jnp.take_along_axis(high[i], spot, axis=1),
                    )
                    total = value if total is None else total + value
                scored = jnp.sum(total, axis=0, keepdims=True)
                out[k, g, b : b + 1] = jnp.where(b < live, scored, 0.0)


def kernel(
    hist_h, act_h, table_h, win_h, wout_h, wint_h, codebook_h, codes_h, cand_h, counts_h,
    out,
    hist, act, table, win, wout, wint, codebook, codes, cand, counts,
    weights, outs, own_rows, got_rows, shard,
    x, normed, proj, attn, codes_got, tables,
    in_sem, mid_sem, late_sem,
    ex_s, ex_r, z_s, z_r, p_s, p1_r, p2_r, f_r, c_s, c_r,
):
    item, fsdp = lax.axis_index("item"), lax.axis_index("fsdp")
    y, x_lo = item // XL, item % XL
    z, x_hi, c = fsdp // (2 * XH), (fsdp // 2) % XH, fsdp % 2
    zq, zr = z // 4, z % 4
    xx = x_hi * XL + x_lo
    s = c * 2 + x_lo
    partner = (item, fsdp + 1 - 2 * c)

    def at_z(to):
        return (item, to * (2 * XH) + x_hi * 2 + c)

    def x_peer(off):
        to = lax.rem(xx + off, XS)
        return (y * XL + to % XL, z * (2 * XH) + (to // XL) * 2 + c)

    def y_peer(off):
        return (lax.rem(y + off, YS) * XL + x_lo, fsdp)

    def copy(src, dst, send, recv, to):
        return pltpu.make_async_remote_copy(
            src_ref=src, dst_ref=dst, send_sem=send, recv_sem=recv, device_id=to, device_id_type=MESH
        )

    barrier = pltpu.get_barrier_semaphore()
    near = [partner] + [x_peer(o) for o in range(1, XS)] + [y_peer(o) for o in range(1, YS)]
    own_quarter = [at_z(zq * ZP + lax.rem(z + o, ZP)) for o in range(1, ZP)]
    sibling = [at_z((zq + 1 - 2 * (zq % 2)) * ZP + t) for t in range(ZP)]
    planes = [at_z(t) for t in range(ZS)]

    def greet(sem, peers):
        for peer in peers:
            pl.semaphore_signal(sem, inc=1, device_id=peer, device_id_type=MESH)

    def if_quarter(which, act):
        pl.when({0: zq == 0, 1: zq == 1, 2: zq >= 2}[which])(act)

    EARLY, MID, LATE = range(3)

    operands = [
        (win_h, win), (wout_h, wout), (wint_h, wint), (hist_h, hist), (act_h, act), (table_h, table),
        (codebook_h, codebook), (codes_h, codes), (cand_h, cand), (counts_h, counts),
    ]
    fetches = [pltpu.make_async_copy(h, v, in_sem.at[i]) for i, (h, v) in enumerate(operands)]
    for t in fetches[:3]:
        t.start()
    greet(barrier, near + own_quarter)
    if_quarter(EARLY, lambda: greet(barrier, planes[ZP:]))
    if_quarter(MID, lambda: greet(barrier, planes[2 * ZP :]))
    if_quarter(LATE, lambda: greet(barrier, sibling))

    for t in fetches[3:]:
        t.start()

    def spread(dst0, value):
        value = value.astype(F32)
        for j in range(value.shape[1] // 128):
            own_rows[dst0 + j] = value[:, j * 128 : (j + 1) * 128]

    fetches[0].wait()
    spread(0, win[0])

    def prepare():
        for t in fetches[3:]:
            t.wait()
        codes_got[y, x_lo, pl.ds(c * 8, 8)] = codes[pl.ds(c * 8, 8)].astype(F32).astype(BF16)
        start_values(hist, act, table, x, normed)

    first = jnp.logical_and(z <= 1, item + fsdp > 0)
    pl.when(first)(prepare)
    count = len(near) + ZP - 1
    if_quarter(EARLY, lambda: pl.semaphore_wait(barrier, count))
    if_quarter(MID, lambda: pl.semaphore_wait(barrier, count + ZP))
    if_quarter(LATE, lambda: pl.semaphore_wait(barrier, count + 3 * ZP))

    spans = [(0, IN_BLKS), (IN_BLKS, ALL_BLKS)]
    trades = [
        copy(own_rows.at[a:b], got_rows.at[a:b], ex_s.at[i], ex_r.at[i], partner)
        for i, (a, b) in enumerate(spans)
    ]
    trades[0].start()

    if_quarter(MID, lambda: greet(mid_sem, planes[:ZP]))
    if_quarter(LATE, lambda: greet(late_sem, planes[: 2 * ZP]))

    spread(IN_BLKS, win[1])
    fetches[1].wait()
    spread(2 * IN_BLKS, wout[0])
    spread(2 * IN_BLKS + OUT_BLKS, wout[1])
    fetches[2].wait()
    spread(2 * IN_BLKS + 2 * OUT_BLKS, wint[...])
    trades[1].start()

    def assemble(a, b):
        for j in range(a, b):
            mine, theirs = own_rows[j], got_rows[j]
            first = jnp.where(c == 0, mine, theirs)
            second = jnp.where(c == 0, theirs, mine)
            shard[j] = jnp.concatenate([first, second], axis=0).astype(BF16)

    blk = jnp.where(c == 0, y * 2 + x_lo, 8 + x_lo * 4 + y)
    shard_outs = shard.at[2 * IN_BLKS :].reshape(3, OUT_BLKS, 16, 128)

    def z_ends(chunk):
        if chunk < 2:
            return shard.at[chunk * IN_BLKS + blk], weights.at[chunk, blk, z, x_hi]
        m = slice(*OUT_PART[chunk])
        return shard_outs.at[m, y], outs.at[m, y, zq, zr, x_hi]

    def z_send(chunk, to):
        copy(*z_ends(chunk), z_s.at[chunk], z_r.at[chunk, zq], at_z(to)).start()

    def z_keep(chunk):
        src, dst = z_ends(chunk)
        pltpu.make_async_copy(src, dst, z_r.at[chunk, zq]).start()

    def if_has(chunk, act):
        if chunk < 2:
            act()
        else:
            pl.when(zr == s)(act)

    def z_to(chunk, first, last):
        def act():
            for t in range(first, last):
                z_send(chunk, t)

        if_has(chunk, act)

    def z_near(chunk):
        if_quarter(MID, lambda: z_to(chunk, 0, ZP))

        def act():
            z_keep(chunk)
            for t in range(ZP - 1):
                z_send(chunk, zq * ZP + t + jnp.where(t >= zr, 1, 0))

            @pl.when(zq >= 2)
            def _():
                for t in range(ZP):
                    z_send(chunk, (zq + 1 - 2 * (zq % 2)) * ZP + t)

        if_has(chunk, act)
        if_quarter(LATE, lambda: z_to(chunk, 0, 2 * ZP))

    def group(chunk, n_in, n_out):
        if chunk < 2:
            return weights.reshape(2 * IN_BLKS * ZS * XH, 16, 128).at[:n_in]
        first, last = OUT_PART[chunk]
        return outs.reshape(3 * OUT_BLKS * ZS * XH, 16, 128).at[: n_out * (last - first)]

    trades[0].wait_recv()
    assemble(*spans[0])
    z_near(0)
    pl.when(zq >= 2)(prepare)
    trades[1].wait_recv()
    assemble(*spans[1])
    for chunk in ORDER[1:]:
        z_near(chunk)

    pl.when(jnp.logical_and(zq <= 1, jnp.logical_not(first)))(prepare)

    other_lo = (item + 1 - 2 * x_lo, fsdp)

    def codes_copy(ref, to, stage):
        return copy(ref, ref, c_s, c_r.at[stage], to)

    def codes_first():
        @pl.when(c == 0)
        def _():
            codes_copy(codes_got.at[y, x_lo, 0:8], other_lo, 0).start()

        @pl.when(c == 1)
        def _():
            for off in (2, 1, 3):
                codes_copy(codes_got.at[y, x_lo, 8:16], y_peer(off), 0).start()

    def codes_second():
        @pl.when(c == 0)
        def _():
            codes_copy(codes_got.at[y, 1 - x_lo, 0:8], partner, 0).wait_recv()
            for off in (2, 1, 3):
                codes_copy(codes_got.at[y, :, 0:8], y_peer(off), 1).start()

        @pl.when(c == 1)
        def _():
            codes_copy(codes_got.at[0:3, 0, 8:16], partner, 0).wait_recv()
            codes_copy(codes_got.at[:, x_lo, 8:16], other_lo, 1).start()

    def codes_third():
        @pl.when(c == 0)
        def _():
            codes_copy(codes_got.at[0:3, :, 0:8], partner, 1).wait_recv()
            codes_copy(codes_got.at[:, :, 0:8], partner, 2).start()

        @pl.when(c == 1)
        def _():
            codes_copy(codes_got.at[:, 0, 8:16], partner, 1).wait_recv()
            codes_copy(codes_got.at[:, :, 8:16], partner, 2).start()

    def codes_last():
        pl.when(c == 0)(lambda: codes_copy(codes_got.at[:, :, 8:16], partner, 2).wait_recv())
        pl.when(c == 1)(lambda: codes_copy(codes_got.at[:, :, 0:8], partner, 2).wait_recv())

    codes_first()

    def first_peer(off):
        xp, yp = x_peer(off), y_peer(off)
        return (jnp.where(c == 0, xp[0], yp[0]), jnp.where(c == 0, xp[1], yp[1]))

    def part(chunk, q):
        if chunk < 2:
            return weights.at[chunk, blk, pl.ds(q * ZP, ZP), x_hi]
        return outs.at[slice(*OUT_PART[chunk]), y, q, s, x_hi]

    def piece(which, chunk, q, off):
        if which == 0:
            at_y = lax.rem(y + YS - off, YS)
            if chunk < 2:
                return weights.at[chunk, pl.ds(at_y * 2, 2), pl.ds(q * ZP, ZP)]
            return outs.at[slice(*OUT_PART[chunk]), at_y, q, 0:2]
        at_x = lax.rem(xx + XS - off, XS)
        lo, hi = at_x % XL, at_x // XL
        if chunk < 2:
            return weights.at[chunk, pl.ds(8 + lo * 4, 4), pl.ds(q * ZP, ZP), hi]
        return outs.at[slice(*OUT_PART[chunk]), :, q, 2 + lo, hi]

    def piece_part(which, chunk, q, off, n):
        ref = piece(which, chunk, q, off)
        if chunk < 2:
            many = 1 if which == 0 else 2
            return ref.at[n * many : (n + 1) * many]
        return ref.at[:, n] if which == 0 else ref.at[:, 2 * n : 2 * n + 2]

    def core_half(which, chunk):
        if chunk < 2:
            return weights.at[chunk, which * 8 : which * 8 + 8]
        return outs.at[slice(*OUT_PART[chunk]), :, :, which * 2 : which * 2 + 2]

    def by_core(act):
        pl.when(c == 0)(lambda: act(0))
        pl.when(c == 1)(lambda: act(1))

    def after_z(chunk, q):
        ref = part(chunk, q)
        copy(ref, ref, p_s.at[chunk], z_r.at[chunk, q], partner).wait_recv()
        for off in (2, 1, 3):
            copy(ref, ref, p_s.at[chunk], p1_r.at[chunk, q], first_peer(off)).start()

    def after_step1(chunk, q, ring=False):
        ref = group(chunk, 3 * ZP, 3)
        copy(ref, ref, p_s.at[chunk], p1_r.at[chunk, q], partner).wait_recv()

        def act(which):
            ref = piece(which, chunk, q, 0)
            peer = y_peer if which == 0 else x_peer
            for off in (1, 3) if ring else (2, 1, 3):
                copy(ref, ref, p_s.at[chunk], p2_r.at[chunk, q, 1 - off % 2], peer(off)).start()
            pass_on(which, chunk, q, 0)

        by_core(act)

    def pass_on(which, chunk, q, off):
        ref = piece(which, chunk, q, off)
        copy(ref, ref, p_s.at[chunk], f_r.at[chunk], partner).start()

    def got_near(chunk, q):
        ref = group(chunk, 8 * ZP, 8)
        copy(ref, ref, p_s.at[chunk], p2_r.at[chunk, q, 0], partner).wait_recv()

    def after_near(chunk, q):
        def act(which):
            peer = y_peer if which == 0 else x_peer
            for off in (1, 3):
                on = piece_part(which, chunk, q, off, off // 2)
                copy(on, on, p_s.at[chunk], p2_r.at[chunk, q, 1], peer(off)).start()
            for off in (1, 3):
                pass_on(which, chunk, q, off)

        got_near(chunk, q)
        by_core(act)

    def after_far(chunk, q):
        def act(which):
            ref = piece(which, chunk, q, 2)
            copy(ref, ref, p_s.at[chunk], p2_r.at[chunk, q, 1], partner).wait_recv()
            pass_on(which, chunk, q, 2)

        by_core(act)

    def after_step2(chunk, q):
        def act(which):
            pass_on(which, chunk, q, 1)
            pass_on(which, chunk, q, 3)

        got_near(chunk, q)
        by_core(act)
        after_far(chunk, q)

    def after_forward(chunk):
        def act(which):
            ref = core_half(1 - which, chunk)
            copy(ref, ref, p_s.at[chunk], f_r.at[chunk], partner).wait_recv()

        by_core(act)

    q0, q1 = zq, zq + 1 - 2 * (zq % 2)
    q2 = 2 * (1 - zq // 2)

    def each(act, *pairs):
        for q, chunk in pairs:
            act(chunk, q)

    def z_of(*pairs):
        each(after_z, *pairs)

    def step1_of(*pairs):
        each(after_step1, *pairs)

    def ring1_of(*pairs):
        each(functools.partial(after_step1, ring=True), *pairs)

    def step2_of(*pairs):
        each(after_step2, *pairs)

    def near_of(*pairs):
        each(after_near, *pairs)

    def far_of(*pairs):
        each(after_far, *pairs)

    own = [(q0, chunk) for chunk in ORDER]
    sib = [(q1, chunk) for chunk in ORDER]

    def both(chunk):
        return (q0, chunk), (q1, chunk)

    def half(chunk):
        return (q2, chunk), (q2 + 1, chunk)

    def late_rows():
        pl.semaphore_wait(late_sem, 2 * ZP)
        z_to(IN0, 2 * ZP, ZS)

    codes_second()

    @pl.when(zq <= 1)
    def _():
        z_of(*own)

        @pl.when(zq == 0)
        def _():
            pl.semaphore_wait(mid_sem, ZP)
            for chunk in ORDER:
                z_to(chunk, ZP, 2 * ZP)

        pl.when(zq == 1)(late_rows)
        ring1_of(*own)
        z_of(*sib)
        pl.when(zq == 0)(late_rows)
        codes_third()
        near_of(*own)
        z_of(*half(IN0))
        step1_of(*sib[:1])
        ring1_of(*sib[1:])
        for chunk in ORDER[1:]:
            z_to(chunk, 2 * ZP, ZS)
        far_of(*own)
        step1_of(*half(IN0))
        z_of(*half(OUT0))
        step2_of(*sib[:1])
        near_of(*sib[1:])
        z_of(*half(IN1))
        step1_of(*half(OUT0))
        step1_of(*half(IN1))
        far_of((q1, OUT0))
        step2_of(*half(IN0))
        z_of(*half(OUT1))
        far_of((q1, IN1), (q1, OUT1))

    def if_late(act):
        pl.when(zq >= 2)(act)

    @if_late
    def _():
        z_of(*both(IN0))
        z_of(*both(OUT0))
        ring1_of(*both(IN0))
        z_of(*both(IN1))
        ring1_of(*both(OUT0))
        codes_third()
        near_of(*both(IN0))
        ring1_of(*both(IN1))
        z_of(*half(IN0))
        near_of(*both(OUT0))
        far_of(*both(IN0))
        z_of(*both(OUT1))
        step1_of(*half(IN0))
        near_of(*both(IN1))
        far_of(*both(OUT0))
        z_of(*half(OUT0))
        z_of(*half(IN1))
        ring1_of(*both(OUT1))
        step1_of(*half(OUT0))
        step1_of(*half(IN1))
        z_of(*half(OUT1))
        far_of(*both(IN1))
        step2_of(*half(IN0))

    for pair in range(4):
        project(0, 4 * c + pair, weights, normed, proj)
    after_forward(IN0)
    for pair in range(4):
        project(0, 4 - 4 * c + pair, weights, normed, proj)

    if_late(lambda: near_of(*both(OUT1)))
    step2_of(*half(OUT0))
    for head in range(HEADS):
        attend(head, proj, attn)
    step1_of(*half(OUT1))
    step2_of(*half(IN1))
    after_forward(OUT0)
    add_out(0, outs, 0, proj, attn, x, normed)
    for pair in range(4):
        project(1, 4 * c + pair, weights, normed, proj)
    after_forward(IN1)
    for pair in range(4):
        project(1, 4 - 4 * c + pair, weights, normed, proj)
    if_late(lambda: far_of(*both(OUT1)))
    step2_of(*half(OUT1))
    for head in range(HEADS):
        attend(head, proj, attn)
    codes_last()
    after_forward(OUT1)
    means = add_out(1, outs, 1, proj, attn, x, normed)

    make_tables(outs, means, codebook, tables)
    score(tables, codes_got, cand, counts, out)

    for t in trades:
        t.wait_send()
    ref = codes_got.reshape(ITEMS * NB, SUB, BS).at[: 15 * 8]
    copy(ref, ref, c_s, c_r.at[0], partner).wait_send()
    for chunk in range(4):

        def left(chunk=chunk):
            ref = group(chunk, ZS - 1, ZS - 1)
            copy(ref, ref, z_s.at[chunk], c_r.at[0], partner).wait_send()

        if_has(chunk, left)
        ref = group(chunk, 4 * 124, 4 * 31)
        copy(ref, ref, p_s.at[chunk], c_r.at[0], partner).wait_send()


def body(history, actions, action_table, w_in, w_out, w_int, codebook, codes, cand, counts):
    hbm = pl.BlockSpec(memory_space=pltpu.HBM)
    dma = pltpu.SemaphoreType.DMA
    operands = (
        history, actions, action_table, w_in, w_out, w_int,
        jnp.transpose(codebook, (0, 2, 1)),
        jnp.transpose(codes, (0, 2, 1)),
        jnp.transpose(cand, (0, 1, 3, 2)),
        counts,
    )
    made = pl.pallas_call(
        kernel,
        out_shape=pltpu.VMEM((INTR, ITEMS, CAND, BS), F32),
        in_specs=[hbm] * 10,
        out_specs=pl.BlockSpec(memory_space=pltpu.VMEM),
        scratch_shapes=[pltpu.VMEM(a.shape, a.dtype) for a in operands[:8]]
        + [pltpu.SMEM(a.shape, a.dtype) for a in operands[8:]]
        + [
            pltpu.VMEM((2, IN_BLKS, ZS, XH, 16, 128), BF16),
            pltpu.VMEM((3, OUT_BLKS, 4, 4, XH, 16, 128), BF16),
            pltpu.VMEM((ALL_BLKS, 8, 128), F32),
            pltpu.VMEM((ALL_BLKS, 8, 128), F32),
            pltpu.VMEM((ALL_BLKS, 16, 128), BF16),
            pltpu.VMEM((L, D), F32),
            pltpu.VMEM((L, D), BF16),
            pltpu.VMEM((IN_BLKS, L, 128), BF16),
            pltpu.VMEM((HEADS, L, HD), F32),
            pltpu.VMEM((YS, XL, NB, SUB, BS), BF16),
            pltpu.VMEM((INTR * SUB, CENT), F32),
            dma((len(operands),)),
            pltpu.SemaphoreType.REGULAR,
            pltpu.SemaphoreType.REGULAR,
            dma((2,)),
            dma((2,)),
            dma((4,)),
            dma((4, 4)),
            dma((4,)),
            dma((4, 4)),
            dma((4, 4, 2)),
            dma((4,)),
            dma(()),
            dma((3,)),
        ],
        compiler_params=pltpu.CompilerParams(
            collective_id=0, has_side_effects=True, vmem_limit_bytes=56 * 1024 * 1024
        ),
        name="encode_and_score",
    )(*operands)
    return made[None]


def solution(mesh):
    placed = (
        P(("item", "fsdp"), None, None),
        P(("item", "fsdp"), None),
        P(),
        P(None, "fsdp", None),
        P(None, "fsdp", None),
        P("fsdp", None),
        P(),
        P("item", None, None),
        P(("item", "fsdp"), None, None, None),
        P(("item", "fsdp"), None),
    )
    return jax.shard_map(
        body,
        mesh=mesh,
        in_specs=placed,
        out_specs=P(("item", "fsdp"), None, None, None, None),
        check_vma=False,
    )
```
